128 devices in a mesh: ctx: 8 (over x, core), head: 16 (over z, y).
Axes of the slice: x: 4, y: 4, z: 4, core: 2. Of those that a mesh axis runs over, the one named last changes fastest.
Arguments:
- features: bfloat16 [2048, 6144], P('ctx', 'head'), may hold values from -6 to 6
- w_query: bfloat16 [6144, 8192], P(None, 'head'), may hold values from -0.078125 to 0.078125
- w_key: bfloat16 [6144, 8192], P(None, 'head'), may hold values from -0.078125 to 0.078125
- w_value: bfloat16 [6144, 8192], P(None, 'head'), may hold values from -0.078125 to 0.078125
- log_decay: float32 [64, 2048], P('head', 'ctx'), may hold values from -1 to 0, as said below
- d_out: bfloat16 [2048, 8192], P('ctx', 'head'), may hold values from -0.011962891 to 0.011962891
Outputs:
- d_features: bfloat16 [2048, 6144], P(('ctx', 'head'))
The draws below stay inside these ranges and needn't reach their ends.
Inputs may be any that keep to these rules, and one draw needn't show every extreme that they name: `log_decay`: entries are negative or zero.
All inputs are finite; a program needn't handle non-finite values.
Results may differ from the reference program's by a relative error of at most 0.023.
Values may be sent and summed in bfloat16 or wider, within the bound.
No kernel may reach another device: no remote copies, remote signals or barrier semaphores. Data moves between devices by JAX's collectives and lax.ppermute only.
A program may use at most 128 MiB of HBM per device.

```python
import jax
import jax.numpy as jnp
from jax import lax

D = 6144
DH = 128
TOK_DEV = 256
HEAD_COUNT = 64
TOKEN_COUNT = 2048


def draw_log_decay(key, part):
    key_collection = jax.random.split(key, 6)
    fast_share = 0.5
    fast_heads = jax.random.uniform(key_collection[0], (HEAD_COUNT, 1), jnp.float32) < fast_share
    fast_rate = jnp.exp(jax.random.uniform(key_collection[1], (HEAD_COUNT, 1), jnp.float32, jnp.log(1.0 / 50.0), jnp.log(1.0 / 30.0)))
    slow_rate = jnp.exp(jax.random.uniform(key_collection[2], (HEAD_COUNT, 1), jnp.float32, jnp.log(0.1), jnp.log(0.5))) / TOKEN_COUNT
    baseline_decay_rate = jnp.where(fast_heads, fast_rate, slow_rate)
    approximate_estimate = jax.random.uniform(key_collection[3], (HEAD_COUNT, TOKEN_COUNT), jnp.float32, 0.5, 1.5)
    token_segments = jax.random.uniform(key_collection[4], (HEAD_COUNT, TOKEN_COUNT), jnp.float32) < 2.0 / TOKEN_COUNT
    segment_length = jnp.log(jax.random.uniform(key_collection[5], (HEAD_COUNT, TOKEN_COUNT), jnp.float32, 0.5, 0.8))
    return -baseline_decay_rate * approximate_estimate + jnp.where(token_segments, segment_length, 0.0)


def level_of(stream_key, extent, cuts, low, largest):
    level, own = 1.0, jax.random.fold_in(stream_key, 6)
    for axis_at, shards_of in cuts:
        steps = jnp.exp(jax.random.uniform(jax.random.fold_in(own, axis_at), (shards_of,), jnp.float32, low / len(cuts), largest / len(cuts)))
        level = level * jnp.repeat(steps, extent[axis_at] // shards_of).reshape([-1 if axis == axis_at else 1 for axis in range(len(extent))])
    return level


def bell_draw(rng, extent, width, bound, cuts=(), kind=jnp.bfloat16):
    gain = level_of(rng, extent, cuts, -0.22, 0.18) if cuts else 1.0
    result = jax.random.normal(rng, extent, jnp.float32) * width * gain
    return jnp.minimum(jnp.maximum(result, -bound), bound).astype(kind)


def setup_inputs(seed: int = 0) -> dict:
    arg_keys = jax.random.split(jax.random.key(seed), 7)
    features = bell_draw(arg_keys[0], (TOKEN_COUNT, D), 1.0, 6.0, ((0, 8), (1, 16)))
    w_query = bell_draw(arg_keys[1], (D, HEAD_COUNT * DH), D ** -0.5, 0.078125, ((1, 16),))
    w_key = bell_draw(arg_keys[2], (D, HEAD_COUNT * DH), D ** -0.5, 0.078125, ((1, 16),))
    w_value = bell_draw(arg_keys[3], (D, HEAD_COUNT * DH), D ** -0.5, 0.078125, ((1, 16),))
    log_decay = draw_log_decay(jax.random.fold_in(arg_keys[6], 71), 0)
    d_out = bell_draw(arg_keys[5], (TOKEN_COUNT, HEAD_COUNT * DH), 0.002, 0.011962891, ((0, 8), (1, 16)))
    return {"features": features, "w_query": w_query, "w_key": w_key, "w_value": w_value, "log_decay": log_decay, "d_out": d_out}


HI = lax.Precision.HIGHEST


def split_heads(flat):
    return flat.reshape(flat.shape[0], -1, DH).transpose(1, 0, 2)


def merge_heads(stacked):
    return stacked.transpose(1, 0, 2).reshape(stacked.shape[1], -1)


def block_factors(decay_b):
    cumul = jnp.cumsum(decay_b, axis=1)
    total = cumul[:, -1]
    row_count = decay_b.shape[1]
    causal = jnp.tril(jnp.ones((row_count, row_count), dtype=bool))
    differ = cumul[:, :, None] - cumul[:, None, :]
    weights = jnp.where(causal[None], jnp.exp(jnp.minimum(differ, 0.0)), 0.0)
    tail = jnp.exp(total[:, None] - cumul)
    leading = jnp.exp(cumul)
    return total, weights, tail, leading


def own_states(queries, keys_b, values_b, grads_b, tail, leading):
    local_state = jnp.einsum("hsi,hsj->hij", keys_b.astype(jnp.float32) * tail[:, :, None], values_b.astype(jnp.float32), precision=HI)
    local_grad = jnp.einsum("hti,htj->hij", queries.astype(jnp.float32) * leading[:, :, None], grads_b.astype(jnp.float32), precision=HI)
    return local_state, local_grad


def block_grads(queries, keys_b, values_b, grads_b, weights, tail, leading, state_in, grad_in):
    f32 = jnp.float32
    scores = (jnp.einsum("hti,hsi->hts", queries, keys_b, preferred_element_type=f32) * weights).astype(jnp.bfloat16)
    mixing = (jnp.einsum("htj,hsj->hts", grads_b, values_b, preferred_element_type=f32) * weights).astype(jnp.bfloat16)
    state_low = state_in.astype(jnp.bfloat16)
    grad_low = grad_in.astype(jnp.bfloat16)
    grad_query = jnp.einsum("hts,hsi->hti", mixing, keys_b, preferred_element_type=f32)
    grad_query = grad_query + leading[:, :, None] * jnp.einsum("htj,hij->hti", grads_b, state_low, preferred_element_type=f32)
    grad_key = jnp.einsum("hts,hti->hsi", mixing, queries, preferred_element_type=f32)
    grad_key = grad_key + tail[:, :, None] * jnp.einsum("hsj,hij->hsi", values_b, grad_low, preferred_element_type=f32)
    grad_value = jnp.einsum("hts,htj->hsj", scores, grads_b, preferred_element_type=f32)
    grad_value = grad_value + tail[:, :, None] * jnp.einsum("hsi,hij->hsj", keys_b, grad_low, preferred_element_type=f32)
    return grad_query.astype(jnp.bfloat16), grad_key.astype(jnp.bfloat16), grad_value.astype(jnp.bfloat16)


def reference(features, w_query, w_key, w_value, log_decay, d_out):
    query_flat = jnp.dot(features, w_query, preferred_element_type=jnp.float32).astype(jnp.bfloat16)
    key_flat = jnp.dot(features, w_key, preferred_element_type=jnp.float32).astype(jnp.bfloat16)
    value_flat = jnp.dot(features, w_value, preferred_element_type=jnp.float32).astype(jnp.bfloat16)
    blocks = TOKEN_COUNT // TOK_DEV
    head_count = log_decay.shape[0]

    def to_blocks(flat):
        return split_heads(flat).reshape(head_count, blocks, TOK_DEV, DH).transpose(1, 0, 2, 3)

    query_blocks = to_blocks(query_flat)
    key_blocks = to_blocks(key_flat)
    value_blocks = to_blocks(value_flat)
    grad_blocks = to_blocks(d_out)
    decay_blocks = log_decay.reshape(head_count, blocks, TOK_DEV).transpose(1, 0, 2)

    def states_of(inputs):
        queries, keys_b, values_b, grads_b, decay_b = inputs
        total, weights_unused, tail, leading = block_factors(decay_b)
        local_state, local_grad = own_states(queries, keys_b, values_b, grads_b, tail, leading)
        return total, local_state, local_grad

    totals, local_states, local_grads = lax.map(states_of, (query_blocks, key_blocks, value_blocks, grad_blocks, decay_blocks))

    def forward_step(carry, inputs):
        total, local_state = inputs
        return jnp.exp(total)[:, None, None] * carry + local_state, carry

    def backward_step(carry, inputs):
        total, local_grad = inputs
        return local_grad + jnp.exp(total)[:, None, None] * carry, carry

    zero_state = jnp.zeros((head_count, DH, DH), jnp.float32)
    last_unused, states_in = lax.scan(forward_step, zero_state, (totals, local_states))
    first_unused, grads_in = lax.scan(backward_step, zero_state, (totals, local_grads), reverse=True)

    def grads_of(inputs):
        queries, keys_b, values_b, grads_b, decay_b, state_in, grad_in = inputs
        total_unused, weights, tail, leading = block_factors(decay_b)
        return block_grads(queries, keys_b, values_b, grads_b, weights, tail, leading, state_in, grad_in)

    grad_q, grad_k, grad_v = lax.map(grads_of, (query_blocks, key_blocks, value_blocks, grad_blocks, decay_blocks, states_in, grads_in))

    def from_blocks(array):
        return merge_heads(array.transpose(1, 0, 2, 3).reshape(head_count, TOKEN_COUNT, DH))

    summed = jnp.dot(from_blocks(grad_q), w_query.T, preferred_element_type=jnp.float32)
    summed = summed + jnp.dot(from_blocks(grad_k), w_key.T, preferred_element_type=jnp.float32)
    summed = summed + jnp.dot(from_blocks(grad_v), w_value.T, preferred_element_type=jnp.float32)
    return summed.astype(jnp.bfloat16)
```

```python
import functools

import jax
import jax.numpy as jnp
from jax import lax
from jax.experimental import pallas as pl
from jax.experimental.pallas import tpu as pltpu
from jax.sharding import PartitionSpec as P

F32, BF16 = jnp.float32, jnp.bfloat16
HI = lax.Precision.HIGHEST
AXES = ("ctx", "head")
REL = (0, 1, 3, 2)
SIDE = 4
DH = 128
MIB = 2**20
VMEM = pl.BlockSpec(memory_space=pltpu.VMEM)
SMEM = pl.BlockSpec(memory_space=pltpu.SMEM)


def device(x, core, z, y):
    return (x * 2 + core) * 16 + z * 4 + y


def everywhere():
    for x in range(4):
        for core in range(2):
            for z in range(4):
                for y in range(4):
                    yield x, core, z, y


def plane_perm(first, offset):
    pairs = []
    for x, core, z, y in everywhere():
        along_y = (core == 0) == first
        to = (z, (y + offset) % 4) if along_y else ((z + offset) % 4, y)
        pairs.append((device(x, core, z, y), device(x, core, *to)))
    return pairs


def core_perm():
    return [(device(x, c, z, y), device(x, 1 - c, z, y)) for x, c, z, y in everywhere()]


def chip_perm(offset):
    return [
        (device(x, c, z, y), device((x + offset) % 4, c, z, y)) for x, c, z, y in everywhere()
    ]


def move(array, pairs):
    return lax.ppermute(array, AXES, pairs)


def params(mib):
    return pltpu.CompilerParams(vmem_limit_bytes=mib * MIB)


def cost(flops, moved):
    return pl.CostEstimate(flops=flops, bytes_accessed=moved, transcendentals=0)


def nt(a, b):
    return lax.dot_general(a, b, (((1,), (1,)), ((), ())), preferred_element_type=F32)


def tn(a, b):
    return lax.dot_general(a, b, (((0,), (0,)), ((), ())), preferred_element_type=F32)


def nn(a, b):
    return jnp.dot(a, b, preferred_element_type=F32)


def decay_kernel(decay_ref, weights_ref, lead_ref, tail_ref):
    heads, rows = decay_ref.shape
    decay = decay_ref[...]
    row = lax.broadcasted_iota(jnp.int32, (rows, rows), 0)
    column = lax.broadcasted_iota(jnp.int32, (rows, rows), 1)
    causal = column <= row
    lower = jnp.where(causal, 1.0, 0.0)
    upright = lax.dot_general(
        lower, decay, (((1,), (1,)), ((), ())), precision=HI, preferred_element_type=F32
    )
    flat = lax.dot_general(
        decay, lower, (((1,), (1,)), ((), ())), precision=HI, preferred_element_type=F32
    )
    for h in range(heads):
        at_t = upright[:, h : h + 1]
        at_s = flat[h : h + 1, :]
        weights_ref[h] = jnp.where(causal, jnp.exp(jnp.minimum(at_t - at_s, 0.0)), 0.0)
        total = flat[h : h + 1, rows - 1 : rows]
        span = slice(h * DH, (h + 1) * DH)
        lead_ref[:, span] = jnp.broadcast_to(jnp.exp(at_t), (rows, DH))
        tail_ref[:, span] = jnp.broadcast_to(jnp.exp(total - at_t), (rows, DH))


def decay_factors(log_decay):
    heads, rows = log_decay.shape
    wide = jax.ShapeDtypeStruct((rows, heads * DH), F32)
    return pl.pallas_call(
        decay_kernel,
        out_shape=(jax.ShapeDtypeStruct((heads, rows, rows), F32), wide, wide),
        in_specs=[VMEM],
        out_specs=(VMEM, VMEM, VMEM),
        compiler_params=params(8),
        cost_estimate=cost(2_000_000, 2_000_000),
        name="decay",
    )(log_decay)


def project_kernel(has_sum, slot, ids_ref, x_ref, *refs):
    sums = refs[:3] if has_sum else None
    weights = refs[3:6] if has_sum else refs[:3]
    outs = refs[-3:]
    width = x_ref.shape[1] // SIDE
    x = x_ref[...]
    starts = [pl.multiple_of(ids_ref[slot * SIDE + j] * width, 128) for j in range(SIDE)]
    for n, (w_ref, out_ref) in enumerate(zip(weights, outs)):
        w = jnp.concatenate([w_ref[pl.ds(s, width), :] for s in starts], axis=0)
        total = nn(x, w)
        if has_sum:
            total = total + sums[n][...]
        out_ref[...] = total.astype(out_ref.dtype)


def project(ids, x, sums, weights, slot, kind):
    rows, columns = x.shape[0], weights[0].shape[1]
    has_sum = sums is not None
    out = jax.ShapeDtypeStruct((rows, columns), kind)
    return pl.pallas_call(
        functools.partial(project_kernel, has_sum, slot),
        out_shape=(out,) * 3,
        in_specs=[SMEM] + [VMEM] * (4 + 3 * has_sum),
        out_specs=(VMEM,) * 3,
        compiler_params=params(12),
        cost_estimate=cost(2 * 3 * rows * x.shape[1] * columns, 6_000_000),
        name="project",
    )(ids, x, *(sums or ()), *weights)


def states_kernel(q_ref, k_ref, v_ref, g_ref, lead_ref, tail_ref, l_ref, m_ref, pay_ref):
    rows, columns = q_ref.shape
    heads = columns // DH
    for h in range(heads):
        c = slice(h * DH, (h + 1) * DH)
        s = slice(h * DH, (h + 1) * DH)
        k = (k_ref[:, c].astype(F32) * tail_ref[:, c]).astype(BF16)
        q = (q_ref[:, c].astype(F32) * lead_ref[:, c]).astype(BF16)
        local = tn(k, v_ref[:, c])
        grad = tn(q, g_ref[:, c])
        l_ref[s, :] = local
        m_ref[s, :] = grad
        pay_ref[s, :] = local.astype(BF16)
        pay_ref[pl.ds(columns + h * DH, DH), :] = grad.astype(BF16)
        own = jnp.broadcast_to(lead_ref[rows - 1 : rows, c], (16, DH))
        pay_ref[pl.ds(2 * columns + h * 16, 16), :] = own.astype(BF16)


def states(q, k, v, g, lead, tail):
    columns = q.shape[1]
    state = jax.ShapeDtypeStruct((columns, DH), F32)
    pay = jax.ShapeDtypeStruct((2 * columns + columns // 8, DH), BF16)
    return pl.pallas_call(
        states_kernel,
        out_shape=(state, state, pay),
        in_specs=[VMEM] * 6,
        out_specs=(VMEM,) * 3,
        compiler_params=params(8),
        cost_estimate=cost(70_000_000, 3_000_000),
        name="states",
    )(q, k, v, g, lead, tail)


def intra_kernel(q_ref, k_ref, v_ref, g_ref, weights_ref, dq_ref, dk_ref, dv_ref):
    for h in range(q_ref.shape[1] // DH):
        c = slice(h * DH, (h + 1) * DH)
        q, k, v, g = q_ref[:, c], k_ref[:, c], v_ref[:, c], g_ref[:, c]
        weights = weights_ref[h]
        scores = (nt(q, k) * weights).astype(BF16)
        mixing = (nt(g, v) * weights).astype(BF16)
        dq_ref[:, c] = nn(mixing, k)
        dk_ref[:, c] = tn(mixing, q)
        dv_ref[:, c] = tn(scores, g)


def intra(q, k, v, g, weights):
    out = jax.ShapeDtypeStruct(q.shape, F32)
    return pl.pallas_call(
        intra_kernel,
        out_shape=(out,) * 3,
        in_specs=[VMEM] * 5,
        out_specs=(VMEM,) * 3,
        compiler_params=params(8),
        cost_estimate=cost(340_000_000, 4_000_000),
        name="intra",
    )(q, k, v, g, weights)


def chip_kernel(place_ref, l_ref, m_ref, lead_ref, peer_ref, *pays):
    columns = l_ref.shape[0]
    rows = lead_ref.shape[0]
    heads = columns // DH
    core, x = place_ref[0], place_ref[1]
    first = core == 0
    for h in range(heads):
        s = slice(h * DH, (h + 1) * DH)
        own_decay = lead_ref[rows - 1 : rows, s]
        peer_decay = peer_ref[pl.ds(2 * columns + h * 16, 16), :].astype(F32)[0:1, :]
        peer_l = peer_ref[s, :].astype(F32)
        peer_m = peer_ref[pl.ds(columns + h * DH, DH), :].astype(F32)
        own_l, own_m = l_ref[s, :], m_ref[s, :]
        chip_l = jnp.where(first, peer_decay * own_l + peer_l, own_decay * peer_l + own_l)
        chip_m = jnp.where(first, own_m + own_decay * peer_m, peer_m + peer_decay * own_m)
        decay = jnp.broadcast_to(own_decay * peer_decay, (16, DH)).astype(BF16)
        for d, pay_ref in enumerate(pays, 1):
            pay_ref[s, :] = jnp.where(x + d < 4, chip_l, chip_m).astype(BF16)
            pay_ref[pl.ds(columns + h * 16, 16), :] = decay


def chip_states(place, own_l, own_m, lead, peer):
    columns = own_l.shape[0]
    pay = jax.ShapeDtypeStruct((columns + columns // 8, DH), BF16)
    return pl.pallas_call(
        chip_kernel,
        out_shape=(pay,) * 3,
        in_specs=[SMEM] + [VMEM] * 4,
        out_specs=(VMEM,) * 3,
        compiler_params=params(8),
        cost_estimate=cost(1_000_000, 2_000_000),
        name="chip_states",
    )(place, own_l, own_m, lead, peer)


def inter_kernel(
    place_ref, ids_ref, q_ref, k_ref, v_ref, g_ref, lead_ref, tail_ref, peer_ref, one_ref, two_ref,
    three_ref, dq_ref, dk_ref, dv_ref, out_ref, whole_ref,
):
    rows, columns = q_ref.shape
    core, x = place_ref[0], place_ref[1]
    first = core == 0
    far = (one_ref, two_ref, three_ref)

    def chance(condition):
        return jnp.where(condition, 1.0, 0.0).astype(F32)

    for h in range(columns // DH):
        c = slice(h * DH, (h + 1) * DH)
        peer_decay = peer_ref[pl.ds(2 * columns + h * 16, 16), :].astype(F32)[0:1, :]
        peer_l = peer_ref[c, :].astype(F32)
        peer_m = peer_ref[pl.ds(columns + h * DH, DH), :].astype(F32)
        one, two, three = (r[c, :].astype(F32) for r in far)
        d_one, d_two, d_three = (
            r[pl.ds(columns + h * 16, 16), :].astype(F32)[0:1, :] for r in far
        )
        before = (
            chance(x >= 1) * one
            + (chance(x >= 2) * d_one) * two
            + (chance(x >= 3) * d_one * d_two) * three
        )
        after = (
            chance(x <= 2) * three
            + (chance(x <= 1) * d_three) * two
            + (chance(x <= 0) * d_three * d_two) * one
        )
        state = jnp.where(first, before, peer_decay * before + peer_l).astype(BF16)
        grad = jnp.where(first, peer_decay * after + peer_m, after).astype(BF16)
        k, v, g = k_ref[:, c], v_ref[:, c], g_ref[:, c]
        lead, tail = lead_ref[:, c], tail_ref[:, c]
        dq = dq_ref[:, c] + lead * nt(g, state)
        dk = dk_ref[:, c] + tail * nt(v, grad)
        dv = dv_ref[:, c] + tail * nn(k, grad)
        for n, result in enumerate((dq, dk, dv)):
            whole_ref[:, pl.ds(n * columns + h * DH, DH)] = result.astype(BF16)
    for n in range(16):
        start = pl.multiple_of(ids_ref[n] * 16, 16)
        out_ref[pl.ds(n * 16, 16), :] = whole_ref[pl.ds(start, 16), :]


def inter(place, ids, q, k, v, g, lead, tail, peer, far, within):
    rows, columns = q.shape
    return pl.pallas_call(
        inter_kernel,
        out_shape=jax.ShapeDtypeStruct((rows, 3 * columns), BF16),
        in_specs=[SMEM] * 2 + [VMEM] * 13,
        out_specs=VMEM,
        scratch_shapes=[pltpu.VMEM((rows, 3 * columns), BF16)],
        compiler_params=params(8),
        cost_estimate=cost(150_000_000, 6_000_000),
        name="inter",
    )(place, ids, q, k, v, g, lead, tail, peer, *far, *within)


def output_kernel(start, tile, d_ref, wq_ref, wk_ref, wv_ref, own_ref, *sends):
    rows = d_ref.shape[0]
    piece = rows // SIDE
    inner = wq_ref.shape[1]
    for n in range(own_ref.shape[1] // tile):
        total = jnp.zeros((rows, tile), F32)
        for part, w_ref in enumerate((wq_ref, wk_ref, wv_ref)):
            total += nt(
                d_ref[:, part * inner : (part + 1) * inner],
                w_ref[pl.ds(start + n * tile, tile), :],
            )
        c = slice(n * tile, (n + 1) * tile)
        own_ref[:, c] = total[:piece]
        for slot, send_ref in enumerate(sends, 1):
            send_ref[:, c] = total[slot * piece : (slot + 1) * piece].astype(BF16)


def output(d, weights, start, width):
    rows = d.shape[0]
    piece = rows // SIDE
    send = jax.ShapeDtypeStruct((piece, width), BF16)
    return pl.pallas_call(
        functools.partial(output_kernel, start, 512),
        out_shape=(jax.ShapeDtypeStruct((piece, width), F32),) + (send,) * 3,
        in_specs=[VMEM] * 4,
        out_specs=(VMEM,) * 4,
        compiler_params=params(12),
        cost_estimate=cost(2 * rows * width * d.shape[1], 6_000_000),
        name="output",
    )(d, *weights)


def add_kernel(own_ref, a_ref, b_ref, c_ref, keep_ref, *sends):
    piece = keep_ref.shape[0]
    total = (
        own_ref[...]
        + a_ref[...].astype(F32)
        + b_ref[...].astype(F32)
        + c_ref[...].astype(F32)
    )
    keep_ref[...] = total[:piece].astype(keep_ref.dtype)
    for slot, send_ref in enumerate(sends, 1):
        send_ref[...] = total[slot * piece : (slot + 1) * piece].astype(BF16)


def add(own, parts, last):
    rows, width = own.shape
    piece = rows if last else rows // SIDE
    keep = jax.ShapeDtypeStruct((piece, width), BF16 if last else F32)
    send = jax.ShapeDtypeStruct((piece, width), BF16)
    count = 0 if last else 3
    return pl.pallas_call(
        add_kernel,
        out_shape=(keep,) + (send,) * count,
        in_specs=[VMEM] * 4,
        out_specs=(VMEM,) * (1 + count),
        compiler_params=params(12),
        cost_estimate=cost(2_000_000, 4_000_000),
        name="add",
    )(own, *parts)


def shards(features, w_query, w_key, w_value, log_decay, d_out):
    weights = (w_query, w_key, w_value)
    ctx, head = lax.axis_index("ctx"), lax.axis_index("head")
    x, core = ctx // 2, ctx % 2
    z, y = head // 4, head % 4
    rel = jnp.array(REL, jnp.int32)
    slot, inner = rel[:, None], rel[None, :]
    ids = jnp.where(
        core == 0,
        (z + slot) % 4 * 4 + (y + inner) % 4,
        (z + inner) % 4 * 4 + (y + slot) % 4,
    ).reshape(16)
    place = jnp.stack([core, x])

    near = [move(features, plane_perm(True, -r)) for r in REL[1:]]
    leading, tail, factors = None, None, None
    factors, lead, tail = decay_factors(log_decay)
    mine = jnp.concatenate([features, *near], axis=1)
    blocks = [move(mine, plane_perm(False, -r)) for r in REL[1:]]
    sums = project(ids, mine, None, weights, 0, F32)
    sums = project(ids, blocks[0], sums, weights, 1, F32)
    sums = project(ids, blocks[1], sums, weights, 2, F32)
    q, k, v = project(ids, blocks[2], sums, weights, 3, BF16)

    own_l, own_m, pay = states(q, k, v, d_out, lead, tail)
    peer = move(pay, core_perm())
    chip = chip_states(place, own_l, own_m, lead, peer)
    far = [move(p, chip_perm(d)) for d, p in enumerate(chip, 1)]
    within = intra(q, k, v, d_out, factors)
    d = inter(place, ids, q, k, v, d_out, lead, tail, peer, far, within)

    width = w_query.shape[0] // 2
    kept = []
    for start in (0, width):
        own, *sends = output(d, weights, start, width)
        parts = [move(s, plane_perm(False, r)) for s, r in zip(sends, REL[1:])]
        kept.append((own, parts))
    results = []
    for own, parts in kept:
        keep, *sends = add(own, parts, False)
        parts = [move(s, plane_perm(True, r)) for s, r in zip(sends, REL[1:])]
        results.append((keep, parts))
    return jnp.concatenate([add(keep, parts, True)[0] for keep, parts in results], axis=1)


def solution(mesh):
    return jax.shard_map(
        shards,
        mesh=mesh,
        in_specs=(
            P("ctx", "head"),
            P(None, "head"),
            P(None, "head"),
            P(None, "head"),
            P("head", "ctx"),
            P("ctx", "head"),
        ),
        out_specs=P(("ctx", "head"), None),
        check_vma=False,
    )
```

```python
import functools

import jax
import jax.numpy as jnp
from jax import lax
from jax.experimental import pallas as pl
from jax.experimental.pallas import tpu as pltpu
from jax.sharding import PartitionSpec as P

F32, BF16 = jnp.float32, jnp.bfloat16
HI = lax.Precision.HIGHEST
AXES = ("ctx", "head")
REL = (0, 1, 3, 2)
SIDE = 4
DH = 128
MIB = 2**20
VMEM = pl.BlockSpec(memory_space=pltpu.VMEM)
HBM = pl.BlockSpec(memory_space=pltpu.HBM)
HALVES = 2


def device(x, core, z, y):
    return (x * 2 + core) * 16 + z * 4 + y


def everywhere():
    for x in range(4):
        for core in range(2):
            for z in range(4):
                for y in range(4):
                    yield x, core, z, y


def plane_perm(first, offset):
    pairs = []
    for x, core, z, y in everywhere():
        along_y = (core == 0) == first
        to = (z, (y + offset) % 4) if along_y else ((z + offset) % 4, y)
        pairs.append((device(x, core, z, y), device(x, core, *to)))
    return pairs


def core_perm():
    return [(device(x, c, z, y), device(x, 1 - c, z, y)) for x, c, z, y in everywhere()]


def chip_perm(offset):
    return [
        (device(x, c, z, y), device((x + offset) % 4, c, z, y)) for x, c, z, y in everywhere()
    ]


def move(array, pairs):
    return lax.ppermute(array, AXES, pairs)


def place():
    ctx, head = lax.axis_index("ctx"), lax.axis_index("head")
    return ctx >> 1, ctx & 1, head >> 2, head & 3


def member(slot, inner):
    _, core, z, y = place()
    first = core == 0
    z = (z + jnp.where(first, REL[slot], REL[inner])) & 3
    y = (y + jnp.where(first, REL[inner], REL[slot])) & 3
    return z * 4 + y


def params(mib):
    return pltpu.CompilerParams(vmem_limit_bytes=mib * MIB)


def cost(flops, moved):
    return pl.CostEstimate(flops=flops, bytes_accessed=moved, transcendentals=0)


def nt(a, b):
    return lax.dot_general(a, b, (((1,), (1,)), ((), ())), preferred_element_type=F32)


def tn(a, b):
    return lax.dot_general(a, b, (((0,), (0,)), ((), ())), preferred_element_type=F32)


def nn(a, b):
    return jnp.dot(a, b, preferred_element_type=F32)


def decay_kernel(decay_ref, weights_ref, lead_ref, tail_ref):
    heads, rows = decay_ref.shape
    decay = decay_ref[...]
    row = lax.broadcasted_iota(jnp.int32, (rows, rows), 0)
    column = lax.broadcasted_iota(jnp.int32, (rows, rows), 1)
    causal = column <= row
    lower = jnp.where(causal, 1.0, 0.0)
    upright = lax.dot_general(
        lower, decay, (((1,), (1,)), ((), ())), precision=HI, preferred_element_type=F32
    )
    flat = lax.dot_general(
        decay, lower, (((1,), (1,)), ((), ())), precision=HI, preferred_element_type=F32
    )
    for h in range(heads):
        at_t = upright[:, h : h + 1]
        at_s = flat[h : h + 1, :]
        weights_ref[h] = jnp.where(causal, jnp.exp(jnp.minimum(at_t - at_s, 0.0)), 0.0)
        total = flat[h : h + 1, rows - 1 : rows]
        span = slice(h * DH, (h + 1) * DH)
        lead_ref[:, span] = jnp.broadcast_to(jnp.exp(at_t), (rows, DH))
        tail_ref[:, span] = jnp.broadcast_to(jnp.exp(total - at_t), (rows, DH))


def decay_factors(log_decay):
    heads, rows = log_decay.shape
    wide = pltpu.VMEM((rows, heads * DH), F32)
    return pl.pallas_call(
        decay_kernel,
        out_shape=(pltpu.VMEM((heads, rows, rows), F32), wide, wide),
        in_specs=[VMEM],
        out_specs=(VMEM, VMEM, VMEM),
        compiler_params=params(8),
        cost_estimate=cost(2_000_000, 2_000_000),
        name="decay",
    )(log_decay)


def load_kernel(*refs):
    count = len(refs) // 2
    sources, targets, done = refs[:count], refs[count:-1], refs[-1]
    pieces = done.shape[0] // count
    copies = []
    for n, (source, target) in enumerate(zip(sources, targets)):
        rows = source.shape[0] // pieces
        for i in range(pieces):
            at = pl.ds(i * rows, rows)
            copies.append(
                pltpu.make_async_copy(source.at[at], target.at[at], done.at[n * pieces + i])
            )
    for copy in copies:
        copy.start()
    for copy in copies:
        copy.wait()


def load(arrays, mib):
    moved = sum(2 * a.size * a.dtype.itemsize for a in arrays)
    return pl.pallas_call(
        load_kernel,
        out_shape=tuple(pltpu.VMEM(a.shape, a.dtype) for a in arrays),
        in_specs=[HBM] * len(arrays),
        out_specs=(VMEM,) * len(arrays),
        scratch_shapes=[pltpu.SemaphoreType.DMA((4 * len(arrays),))],
        compiler_params=params(mib),
        cost_estimate=cost(0, moved),
        name="load",
    )(*arrays)


def join_kernel(*refs):
    pieces, outs = refs[:SIDE], refs[-HALVES:]
    width = pieces[0].shape[1]
    for n, ref in enumerate(pieces):
        for m, out_ref in enumerate(outs):
            rows = out_ref.shape[0]
            out_ref[:, n * width : (n + 1) * width] = ref[m * rows : (m + 1) * rows, :]


def join(pieces, after):
    rows, width = pieces[0].shape
    return pl.pallas_call(
        join_kernel,
        out_shape=(pltpu.VMEM((rows // HALVES, SIDE * width), BF16),) * HALVES,
        in_specs=[VMEM] * (SIDE + len(after)),
        out_specs=(VMEM,) * HALVES,
        compiler_params=params(4),
        cost_estimate=cost(0, 2_000_000),
        name="join",
    )(*pieces, *after)


def project_kernel(slots, has_sum, *refs):
    count = HALVES * len(slots)
    xs, refs = refs[:count], refs[count:]
    sums, refs = (refs[:3], refs[3:]) if has_sum else (None, refs)
    weights, outs = refs[:3], refs[-3:]
    for n, (w_ref, out_ref) in enumerate(zip(weights, outs)):
        total = sums[n][...] if has_sum else None
        for m, slot in enumerate(slots):
            x = jnp.concatenate([r[...] for r in xs[m * HALVES : (m + 1) * HALVES]], axis=0)
            width = x.shape[1] // SIDE
            starts = [pl.multiple_of(member(slot, j) * width, 128) for j in range(SIDE)]
            w = jnp.concatenate([w_ref[pl.ds(s, width), :] for s in starts], axis=0)
            term = nn(x, w)
            total = term if total is None else total + term
        out_ref[...] = total.astype(out_ref.dtype)


def project(xs, slots, sums, weights, kind, after=()):
    rows, columns = HALVES * xs[0].shape[0], weights[0].shape[1]
    inner = xs[0].shape[1] * len(slots)
    has_sum = sums is not None
    return pl.pallas_call(
        functools.partial(project_kernel, slots, has_sum),
        out_shape=(pltpu.VMEM((rows, columns), kind),) * 3,
        in_specs=[VMEM] * (len(xs) + 3 + 3 * has_sum + len(after)),
        out_specs=(VMEM,) * 3,
        compiler_params=params(12),
        cost_estimate=cost(2 * 3 * rows * inner * columns, 4_000 * inner),
        name="project",
    )(*xs, *(sums or ()), *weights, *after)


def states_kernel(q_ref, k_ref, v_ref, g_ref, lead_ref, tail_ref, l_ref, m_ref, pay_ref):
    rows, columns = q_ref.shape
    heads = columns // DH
    for h in range(heads):
        c = slice(h * DH, (h + 1) * DH)
        s = slice(h * DH, (h + 1) * DH)
        k = (k_ref[:, c].astype(F32) * tail_ref[:, c]).astype(BF16)
        q = (q_ref[:, c].astype(F32) * lead_ref[:, c]).astype(BF16)
        local = tn(k, v_ref[:, c])
        grad = tn(q, g_ref[:, c])
        l_ref[s, :] = local
        m_ref[s, :] = grad
        pay_ref[s, :] = local.astype(BF16)
        pay_ref[pl.ds(columns + h * DH, DH), :] = grad.astype(BF16)
        own = jnp.broadcast_to(lead_ref[rows - 1 : rows, c], (16, DH))
        pay_ref[pl.ds(2 * columns + h * 16, 16), :] = own.astype(BF16)


def states(q, k, v, g, lead, tail):
    columns = q.shape[1]
    state = pltpu.VMEM((columns, DH), F32)
    pay = pltpu.VMEM((2 * columns + columns // 8, DH), BF16)
    return pl.pallas_call(
        states_kernel,
        out_shape=(state, state, pay),
        in_specs=[VMEM] * 6,
        out_specs=(VMEM,) * 3,
        compiler_params=params(8),
        cost_estimate=cost(70_000_000, 3_000_000),
        name="states",
    )(q, k, v, g, lead, tail)


def intra_kernel(q_ref, k_ref, v_ref, g_ref, weights_ref, dq_ref, dk_ref, dv_ref):
    for h in range(q_ref.shape[1] // DH):
        c = slice(h * DH, (h + 1) * DH)
        q, k, v, g = q_ref[:, c], k_ref[:, c], v_ref[:, c], g_ref[:, c]
        weights = weights_ref[h]
        scores = (nt(q, k) * weights).astype(BF16)
        mixing = (nt(g, v) * weights).astype(BF16)
        dq_ref[:, c] = nn(mixing, k)
        dk_ref[:, c] = tn(mixing, q)
        dv_ref[:, c] = tn(scores, g)


def intra(q, k, v, g, weights):
    out = pltpu.VMEM(q.shape, F32)
    return pl.pallas_call(
        intra_kernel,
        out_shape=(out,) * 3,
        in_specs=[VMEM] * 5,
        out_specs=(VMEM,) * 3,
        compiler_params=params(8),
        cost_estimate=cost(340_000_000, 4_000_000),
        name="intra",
    )(q, k, v, g, weights)


def chip_kernel(l_ref, m_ref, lead_ref, peer_ref, *pays):
    columns = l_ref.shape[0]
    rows = lead_ref.shape[0]
    heads = columns // DH
    x, core, _, _ = place()
    first = core == 0
    for h in range(heads):
        s = slice(h * DH, (h + 1) * DH)
        own_decay = lead_ref[rows - 1 : rows, s]
        peer_decay = peer_ref[pl.ds(2 * columns + h * 16, 16), :].astype(F32)[0:1, :]
        peer_l = peer_ref[s, :].astype(F32)
        peer_m = peer_ref[pl.ds(columns + h * DH, DH), :].astype(F32)
        own_l, own_m = l_ref[s, :], m_ref[s, :]
        chip_l = jnp.where(first, peer_decay * own_l + peer_l, own_decay * peer_l + own_l)
        chip_m = jnp.where(first, own_m + own_decay * peer_m, peer_m + peer_decay * own_m)
        decay = jnp.broadcast_to(own_decay * peer_decay, (16, DH)).astype(BF16)
        for d, pay_ref in enumerate(pays, 1):
            pay_ref[s, :] = jnp.where(x + d < 4, chip_l, chip_m).astype(BF16)
            pay_ref[pl.ds(columns + h * 16, 16), :] = decay


def chip_states(own_l, own_m, lead, peer):
    columns = own_l.shape[0]
    pay = pltpu.VMEM((columns + columns // 8, DH), BF16)
    return pl.pallas_call(
        chip_kernel,
        out_shape=(pay,) * 3,
        in_specs=[VMEM] * 4,
        out_specs=(VMEM,) * 3,
        compiler_params=params(8),
        cost_estimate=cost(1_000_000, 2_000_000),
        name="chip_states",
    )(own_l, own_m, lead, peer)


def inter_kernel(
    q_ref, k_ref, v_ref, g_ref, lead_ref, tail_ref, peer_ref, one_ref, two_ref, three_ref,
    dq_ref, dk_ref, dv_ref, out_ref, whole_ref,
):
    rows, columns = q_ref.shape
    x, core, _, _ = place()
    first = core == 0
    far = (one_ref, two_ref, three_ref)

    def chance(condition):
        return jnp.where(condition, 1.0, 0.0).astype(F32)

    for h in range(columns // DH):
        c = slice(h * DH, (h + 1) * DH)
        peer_decay = peer_ref[pl.ds(2 * columns + h * 16, 16), :].astype(F32)[0:1, :]
        peer_l = peer_ref[c, :].astype(F32)
        peer_m = peer_ref[pl.ds(columns + h * DH, DH), :].astype(F32)
        one, two, three = (r[c, :].astype(F32) for r in far)
        d_one, d_two, d_three = (
            r[pl.ds(columns + h * 16, 16), :].astype(F32)[0:1, :] for r in far
        )
        before = (
            chance(x >= 1) * one
            + (chance(x >= 2) * d_one) * two
            + (chance(x >= 3) * d_one * d_two) * three
        )
        after = (
            chance(x <= 2) * three
            + (chance(x <= 1) * d_three) * two
            + (chance(x <= 0) * d_three * d_two) * one
        )
        state = jnp.where(first, before, peer_decay * before + peer_l).astype(BF16)
        grad = jnp.where(first, peer_decay * after + peer_m, after).astype(BF16)
        k, v, g = k_ref[:, c], v_ref[:, c], g_ref[:, c]
        lead, tail = lead_ref[:, c], tail_ref[:, c]
        dq = dq_ref[:, c] + lead * nt(g, state)
        dk = dk_ref[:, c] + tail * nt(v, grad)
        dv = dv_ref[:, c] + tail * nn(k, grad)
        for n, result in enumerate((dq, dk, dv)):
            whole_ref[:, pl.ds(n * columns + h * DH, DH)] = result.astype(BF16)
    for n in range(SIDE * SIDE):
        start = pl.multiple_of(member(n // SIDE, n % SIDE) * 16, 16)
        out_ref[pl.ds(n * 16, 16), :] = whole_ref[pl.ds(start, 16), :]


def inter(q, k, v, g, lead, tail, peer, far, within):
    rows, columns = q.shape
    return pl.pallas_call(
        inter_kernel,
        out_shape=pltpu.VMEM((rows, 3 * columns), BF16),
        in_specs=[VMEM] * 13,
        out_specs=VMEM,
        scratch_shapes=[pltpu.VMEM((rows, 3 * columns), BF16)],
        compiler_params=params(8),
        cost_estimate=cost(150_000_000, 6_000_000),
        name="inter",
    )(q, k, v, g, lead, tail, peer, *far, *within)


def output_kernel(start, tile, d_ref, wq_ref, wk_ref, wv_ref, *refs):
    outs = refs[-SIDE:]
    rows = d_ref.shape[0]
    piece = rows // SIDE
    inner = wq_ref.shape[1]
    for n in range(outs[0].shape[1] // tile):
        total = jnp.zeros((rows, tile), F32)
        for part, w_ref in enumerate((wq_ref, wk_ref, wv_ref)):
            total += nt(
                d_ref[:, part * inner : (part + 1) * inner],
                w_ref[pl.ds(start + n * tile, tile), :],
            )
        c = slice(n * tile, (n + 1) * tile)
        for slot, out_ref in enumerate(outs):
            out_ref[:, c] = total[slot * piece : (slot + 1) * piece].astype(out_ref.dtype)


def output(d, weights, start, width, kinds, after=()):
    rows = d.shape[0]
    return pl.pallas_call(
        functools.partial(output_kernel, start, 512),
        out_shape=tuple(pltpu.VMEM((rows // SIDE, width), kind) for kind in kinds),
        in_specs=[VMEM] * (4 + len(after)),
        out_specs=(VMEM,) * SIDE,
        compiler_params=params(12),
        cost_estimate=cost(2 * rows * width * d.shape[1], 6_000_000),
        name="output",
    )(d, *weights, *after)


def relay_kernel(own_ref, other_ref, *refs):
    out_ref = refs[-1]
    out_ref[...] = (own_ref[...] + other_ref[...].astype(F32)).astype(BF16)


def relay(own, other, after=()):
    return pl.pallas_call(
        relay_kernel,
        out_shape=pltpu.VMEM(own.shape, BF16),
        in_specs=[VMEM] * (2 + len(after)),
        out_specs=VMEM,
        compiler_params=params(4),
        cost_estimate=cost(0, 100_000),
        name="relay",
    )(own, other, *after)


def total_of(own_ref, parts):
    total = own_ref[...]
    for ref in parts:
        total = total + ref[...].astype(F32)
    return total


def add_kernel(terms, *refs):
    own_ref, *parts = refs[:terms]
    earlier, outs = refs[terms:-SIDE], refs[-SIDE:]
    piece, width = outs[0].shape
    total = total_of(own_ref, parts)
    c = slice(width - own_ref.shape[1], width)
    for slot, out_ref in enumerate(outs):
        if earlier:
            out_ref[:, : c.start] = earlier[slot][...]
        out_ref[:, c] = total[slot * piece : (slot + 1) * piece].astype(out_ref.dtype)


def add(half, earlier=()):
    rows, width = half[0].shape
    piece = rows // SIDE
    width += earlier[0].shape[1] if earlier else 0
    return pl.pallas_call(
        functools.partial(add_kernel, len(half)),
        out_shape=(pltpu.VMEM((piece, width), F32),) + (pltpu.VMEM((piece, width), BF16),) * 3,
        in_specs=[VMEM] * (len(half) + len(earlier)),
        out_specs=(VMEM,) * SIDE,
        compiler_params=params(8),
        cost_estimate=cost(0, 500_000),
        name="add",
    )(*half, *earlier)


def finish_kernel(own_ref, a_ref, b_ref, c_ref, out_ref):
    out_ref[...] = total_of(own_ref, (a_ref, b_ref, c_ref)).astype(BF16)


def finish(own, parts):
    return pl.pallas_call(
        finish_kernel,
        out_shape=jax.ShapeDtypeStruct(own.shape, BF16),
        in_specs=[VMEM] * SIDE,
        out_specs=VMEM,
        compiler_params=params(8),
        cost_estimate=cost(500_000, 1_000_000),
        name="finish",
    )(own, *parts)


def near_move(array, offset):
    return move(array, plane_perm(True, offset))


def wide_move(array, offset):
    return move(array, plane_perm(False, offset))


def shards(features, w_query, w_key, w_value, log_decay, d_out):
    near = [near_move(features, -r) for r in REL[1:]]
    own, *weights = load((features, w_query, w_key), 48)
    top, low = join((own, *near), (weights[0],))
    weights, g = (*weights, w_value), d_out
    next_top, last_low = wide_move(top, -1), wide_move(low, 1)
    next_low, last_top = wide_move(low, -1), wide_move(top, 1)
    far_top, far_low = wide_move(next_top, -1), wide_move(last_low, 1)
    factors, lead, tail = decay_factors(log_decay)
    sums = project((top, low), (0,), None, weights, F32, (lead,))
    sums = project((next_top, next_low), (1,), sums, weights, F32)
    sums = project((last_top, last_low), (2,), sums, weights, F32)
    q, k, v = project((far_top, far_low), (3,), sums, weights, BF16)

    own_l, own_m, pay = states(q, k, v, g, lead, tail)
    peer = move(pay, core_perm())
    chip = chip_states(own_l, own_m, lead, peer)
    far = [move(p, chip_perm(d)) for d, p in enumerate(chip, 1)]
    within = intra(q, k, v, g, factors)
    d = inter(q, k, v, g, lead, tail, peer, far, within)

    width = w_query.shape[0] // HALVES
    a_own, a_next, a_last, a_far = output(d, weights, 0, width, (F32, F32, BF16, BF16))
    b_own, b_next, b_last, b_far = output(d, weights, width, width, (F32, BF16, F32, BF16), (a_own,))
    a_last, a_far = wide_move(a_last, -1), wide_move(a_far, 1)
    b_next, b_far = wide_move(b_next, 1), wide_move(b_far, -1)
    a_next = relay(a_next, a_far)
    b_last = relay(b_last, b_far, (a_next,))
    a_next, b_last = wide_move(a_next, 1), wide_move(b_last, -1)
    keep, *sends = add((b_own, b_next, b_last), add((a_own, a_last, a_next)))
    return finish(keep, [near_move(s, r) for s, r in zip(sends, REL[1:])])


def solution(mesh):
    return jax.shard_map(
        shards,
        mesh=mesh,
        in_specs=(
            P("ctx", "head"),
            P(None, "head"),
            P(None, "head"),
            P(None, "head"),
            P("head", "ctx"),
            P("ctx", "head"),
        ),
        out_specs=P(("ctx", "head"), None),
        check_vma=False,
    )
```

```python
import functools

import jax
import jax.numpy as jnp
from jax import lax
from jax.experimental import pallas as pl
from jax.experimental.pallas import tpu as pltpu
from jax.sharding import PartitionSpec as P

F32, BF16 = jnp.float32, jnp.bfloat16
HI = lax.Precision.HIGHEST
AXES = ("ctx", "head")
REL = (0, 1, 3, 2)
SIDE = 4
DH = 128
MIB = 2**20
VMEM = pl.BlockSpec(memory_space=pltpu.VMEM)
HBM = pl.BlockSpec(memory_space=pltpu.HBM)
HALVES = 2


def device(x, core, z, y):
    return (x * 2 + core) * 16 + z * 4 + y


def everywhere():
    for x in range(4):
        for core in range(2):
            for z in range(4):
                for y in range(4):
                    yield x, core, z, y


def plane_perm(first, offset):
    pairs = []
    for x, core, z, y in everywhere():
        along_y = (core == 0) == first
        to = (z, (y + offset) % 4) if along_y else ((z + offset) % 4, y)
        pairs.append((device(x, core, z, y), device(x, core, *to)))
    return pairs


def core_perm():
    return [(device(x, c, z, y), device(x, 1 - c, z, y)) for x, c, z, y in everywhere()]


def chip_perm(offset):
    return [
        (device(x, c, z, y), device((x + offset) % 4, c, z, y)) for x, c, z, y in everywhere()
    ]


def move(array, pairs):
    return lax.ppermute(array, AXES, pairs)


def place():
    ctx, head = lax.axis_index("ctx"), lax.axis_index("head")
    return ctx >> 1, ctx & 1, head >> 2, head & 3


def member(slot, inner):
    _, core, z, y = place()
    first = core == 0
    z = (z + jnp.where(first, REL[slot], REL[inner])) & 3
    y = (y + jnp.where(first, REL[inner], REL[slot])) & 3
    return z * 4 + y


def params(mib):
    return pltpu.CompilerParams(vmem_limit_bytes=mib * MIB)


def cost(flops, moved):
    return pl.CostEstimate(flops=flops, bytes_accessed=moved, transcendentals=0)


def nt(a, b):
    return lax.dot_general(a, b, (((1,), (1,)), ((), ())), preferred_element_type=F32)


def tn(a, b):
    return lax.dot_general(a, b, (((0,), (0,)), ((), ())), preferred_element_type=F32)


def nn(a, b):
    return jnp.dot(a, b, preferred_element_type=F32)


def decay_kernel(decay_ref, weights_ref, lead_ref, tail_ref):
    heads, rows = decay_ref.shape
    decay = decay_ref[...]
    row = lax.broadcasted_iota(jnp.int32, (rows, rows), 0)
    column = lax.broadcasted_iota(jnp.int32, (rows, rows), 1)
    causal = column <= row
    lower = jnp.where(causal, 1.0, 0.0)
    upright = lax.dot_general(
        lower, decay, (((1,), (1,)), ((), ())), precision=HI, preferred_element_type=F32
    )
    flat = lax.dot_general(
        decay, lower, (((1,), (1,)), ((), ())), precision=HI, preferred_element_type=F32
    )
    for h in range(heads):
        at_t = upright[:, h : h + 1]
        at_s = flat[h : h + 1, :]
        weights_ref[h] = jnp.where(causal, jnp.exp(jnp.minimum(at_t - at_s, 0.0)), 0.0)
        total = flat[h : h + 1, rows - 1 : rows]
        span = slice(h * DH, (h + 1) * DH)
        lead_ref[:, span] = jnp.broadcast_to(jnp.exp(at_t), (rows, DH))
        tail_ref[:, span] = jnp.broadcast_to(jnp.exp(total - at_t), (rows, DH))


def decay_factors(log_decay):
    heads, rows = log_decay.shape
    wide = pltpu.VMEM((rows, heads * DH), F32)
    return pl.pallas_call(
        decay_kernel,
        out_shape=(pltpu.VMEM((heads, rows, rows), F32), wide, wide),
        in_specs=[VMEM],
        out_specs=(VMEM, VMEM, VMEM),
        compiler_params=params(8),
        cost_estimate=cost(2_000_000, 2_000_000),
        name="decay",
    )(log_decay)


def load_kernel(*refs):
    count = len(refs) // 2
    sources, targets, done = refs[:count], refs[count:-1], refs[-1]
    pieces = done.shape[0] // count
    copies = []
    for n, (source, target) in enumerate(zip(sources, targets)):
        rows = source.shape[0] // pieces
        for i in range(pieces):
            at = pl.ds(i * rows, rows)
            copies.append(
                pltpu.make_async_copy(source.at[at], target.at[at], done.at[n * pieces + i])
            )
    for copy in copies:
        copy.start()
    for copy in copies:
        copy.wait()


def load(arrays, mib):
    moved = sum(2 * a.size * a.dtype.itemsize for a in arrays)
    return pl.pallas_call(
        load_kernel,
        out_shape=tuple(pltpu.VMEM(a.shape, a.dtype) for a in arrays),
        in_specs=[HBM] * len(arrays),
        out_specs=(VMEM,) * len(arrays),
        scratch_shapes=[pltpu.SemaphoreType.DMA((4 * len(arrays),))],
        compiler_params=params(mib),
        cost_estimate=cost(0, moved),
        name="load",
    )(*arrays)


def join_kernel(*refs):
    pieces, outs = refs[:SIDE], refs[-HALVES:]
    width = pieces[0].shape[1]
    for n, ref in enumerate(pieces):
        for m, out_ref in enumerate(outs):
            rows = out_ref.shape[0]
            out_ref[:, n * width : (n + 1) * width] = ref[m * rows : (m + 1) * rows, :]


def join(pieces, after):
    rows, width = pieces[0].shape
    return pl.pallas_call(
        join_kernel,
        out_shape=(pltpu.VMEM((rows // HALVES, SIDE * width), BF16),) * HALVES,
        in_specs=[VMEM] * (SIDE + len(after)),
        out_specs=(VMEM,) * HALVES,
        compiler_params=params(4),
        cost_estimate=cost(0, 2_000_000),
        name="join",
    )(*pieces, *after)


def project_kernel(slots, has_sum, *refs):
    count = HALVES * len(slots)
    xs, refs = refs[:count], refs[count:]
    sums, refs = (refs[:3], refs[3:]) if has_sum else (None, refs)
    weights, outs = refs[:3], refs[-3:]
    for n, (w_ref, out_ref) in enumerate(zip(weights, outs)):
        total = sums[n][...] if has_sum else None
        for m, slot in enumerate(slots):
            x = jnp.concatenate([r[...] for r in xs[m * HALVES : (m + 1) * HALVES]], axis=0)
            width = x.shape[1] // SIDE
            starts = [pl.multiple_of(member(slot, j) * width, 128) for j in range(SIDE)]
            w = jnp.concatenate([w_ref[pl.ds(s, width), :] for s in starts], axis=0)
            term = nn(x, w)
            total = term if total is None else total + term
        out_ref[...] = total.astype(out_ref.dtype)


def project(xs, slots, sums, weights, kind, after=()):
    rows, columns = HALVES * xs[0].shape[0], weights[0].shape[1]
    inner = xs[0].shape[1] * len(slots)
    has_sum = sums is not None
    return pl.pallas_call(
        functools.partial(project_kernel, slots, has_sum),
        out_shape=(pltpu.VMEM((rows, columns), kind),) * 3,
        in_specs=[VMEM] * (len(xs) + 3 + 3 * has_sum + len(after)),
        out_specs=(VMEM,) * 3,
        compiler_params=params(12),
        cost_estimate=cost(2 * 3 * rows * inner * columns, 4_000 * inner),
        name="project",
    )(*xs, *(sums or ()), *weights, *after)


def stack(lines):
    row = lax.broadcasted_iota(jnp.int32, (16, DH), 0)
    block = jnp.zeros((16, DH), F32)
    for n, line in enumerate(lines):
        block = jnp.where(row == n, line, block)
    return block.astype(BF16)


def line_of(ref, start, n):
    return ref[pl.ds(start, 16), :].astype(F32)[n : n + 1, :]


def states_kernel(q_ref, k_ref, v_ref, g_ref, lead_ref, tail_ref, l_ref, m_ref, pay_ref):
    rows, columns = q_ref.shape
    heads = columns // DH
    local, grad = [], []
    for h in range(heads):
        c = slice(h * DH, (h + 1) * DH)
        k = (k_ref[:, c].astype(F32) * tail_ref[:, c]).astype(BF16)
        q = (q_ref[:, c].astype(F32) * lead_ref[:, c]).astype(BF16)
        local.append(tn(k, v_ref[:, c]))
        grad.append(tn(q, g_ref[:, c]))
    first = place()[1] == 0
    half = heads // 2
    for i in range(half):
        s = slice(i * DH, (i + 1) * DH)
        for ref, state, at in ((l_ref, local, i), (m_ref, grad, half + i)):
            low, high = state[i], state[half + i]
            ref[s, :] = jnp.where(first, low, high)
            pay_ref[at * DH : (at + 1) * DH, :] = jnp.where(first, high, low).astype(BF16)
    pay_ref[pl.ds(columns, 16), :] = stack(
        [lead_ref[rows - 1 : rows, h * DH : (h + 1) * DH] for h in range(heads)]
    )


def states(q, k, v, g, lead, tail):
    columns = q.shape[1]
    state = pltpu.VMEM((columns // 2, DH), F32)
    return pl.pallas_call(
        states_kernel,
        out_shape=(state, state, pltpu.VMEM((columns + 16, DH), BF16)),
        in_specs=[VMEM] * 6,
        out_specs=(VMEM,) * 3,
        compiler_params=params(8),
        cost_estimate=cost(70_000_000, 3_000_000),
        name="states",
    )(q, k, v, g, lead, tail)


def intra_kernel(q_ref, k_ref, v_ref, g_ref, weights_ref, dq_ref, dk_ref, dv_ref):
    for h in range(q_ref.shape[1] // DH):
        c = slice(h * DH, (h + 1) * DH)
        q, k, v, g = q_ref[:, c], k_ref[:, c], v_ref[:, c], g_ref[:, c]
        weights = weights_ref[h]
        scores = (nt(q, k) * weights).astype(BF16)
        mixing = (nt(g, v) * weights).astype(BF16)
        dq_ref[:, c] = nn(mixing, k)
        dk_ref[:, c] = tn(mixing, q)
        dv_ref[:, c] = tn(scores, g)


def intra(q, k, v, g, weights):
    out = pltpu.VMEM(q.shape, F32)
    return pl.pallas_call(
        intra_kernel,
        out_shape=(out,) * 3,
        in_specs=[VMEM] * 5,
        out_specs=(VMEM,) * 3,
        compiler_params=params(8),
        cost_estimate=cost(340_000_000, 4_000_000),
        name="intra",
    )(q, k, v, g, weights)


def pair_of(l_ref, m_ref, lead_ref, peer_ref):
    columns, rows = peer_ref.shape[0] - 16, lead_ref.shape[0]
    half = columns // DH // 2
    first = place()[1] == 0
    for i in range(half):
        s = slice(i * DH, (i + 1) * DH)
        own, other = (
            jnp.where(first, line(i), line(half + i))
            for line in (
                lambda h: lead_ref[rows - 1 : rows, h * DH : (h + 1) * DH],
                lambda h: line_of(peer_ref, columns, h),
            )
        )
        peer_l = peer_ref[s, :].astype(F32)
        peer_m = peer_ref[(half + i) * DH : (half + i + 1) * DH, :].astype(F32)
        yield i, (l_ref[s, :], peer_l), (m_ref[s, :], peer_m), (own, other)


def chip_kernel(l_ref, m_ref, lead_ref, peer_ref, *pays):
    x, core, _, _ = place()
    first = core == 0
    decays = []
    rows = pays[0].shape[0] - 16
    for i, (own_l, peer_l), (own_m, peer_m), (own, other) in pair_of(l_ref, m_ref, lead_ref, peer_ref):
        chip_l = jnp.where(first, other * own_l + peer_l, own * peer_l + own_l)
        chip_m = jnp.where(first, own_m + own * peer_m, peer_m + other * own_m)
        decays.append(own * other)
        for d, pay_ref in enumerate(pays, 1):
            both = jnp.where(x + d < 4, chip_l, chip_m)
            pay_ref[i * DH : (i + 1) * DH, :] = both.astype(BF16)
    for pay_ref in pays:
        pay_ref[pl.ds(rows, 16), :] = stack(decays)


def chip_states(own_l, own_m, lead, peer):
    pay = pltpu.VMEM((own_l.shape[0] + 16, DH), BF16)
    return pl.pallas_call(
        chip_kernel,
        out_shape=(pay,) * 3,
        in_specs=[VMEM] * 4,
        out_specs=(VMEM,) * 3,
        compiler_params=params(8),
        cost_estimate=cost(500_000, 1_000_000),
        name="chip_states",
    )(own_l, own_m, lead, peer)


def outer_kernel(l_ref, m_ref, lead_ref, peer_ref, one_ref, two_ref, three_ref, *refs):
    mine_ref, theirs_ref = refs[-2:]
    x, core, _, _ = place()
    first = core == 0
    far = (one_ref, two_ref, three_ref)
    rows = one_ref.shape[0] - 16

    def chance(condition):
        return jnp.where(condition, 1.0, 0.0).astype(F32)

    for i, (own_l, peer_l), (own_m, peer_m), (own, other) in pair_of(l_ref, m_ref, lead_ref, peer_ref):
        s = slice(i * DH, (i + 1) * DH)
        one, two, three = (r[s, :].astype(F32) for r in far)
        d_one, _, d_three = (line_of(r, rows, i) for r in far)
        d_two = line_of(two_ref, rows, i)
        before = (
            chance(x >= 1) * one
            + (chance(x >= 2) * d_one) * two
            + (chance(x >= 3) * d_one * d_two) * three
        )
        after = (
            chance(x <= 2) * three
            + (chance(x <= 1) * d_three) * two
            + (chance(x <= 0) * d_three * d_two) * one
        )
        low_decay, high_decay = jnp.where(first, own, other), jnp.where(first, other, own)
        low_l, high_m = jnp.where(first, own_l, peer_l), jnp.where(first, peer_m, own_m)
        low = (before, high_decay * after + high_m)
        high = (low_decay * before + low_l, after)
        for n in range(2):
            at = slice(n * rows + i * DH, n * rows + (i + 1) * DH)
            mine_ref[at, :] = jnp.where(first, low[n], high[n]).astype(BF16)
            theirs_ref[at, :] = jnp.where(first, high[n], low[n]).astype(BF16)


def outer_states(own_l, own_m, lead, peer, far, after):
    out = pltpu.VMEM((2 * own_l.shape[0], DH), BF16)
    return pl.pallas_call(
        outer_kernel,
        out_shape=(out, out),
        in_specs=[VMEM] * (7 + len(after)),
        out_specs=(VMEM,) * 2,
        compiler_params=params(8),
        cost_estimate=cost(500_000, 1_000_000),
        name="outer_states",
    )(own_l, own_m, lead, peer, *far, *after)


def inter_kernel(
    q_ref, k_ref, v_ref, g_ref, lead_ref, tail_ref, mine_ref, theirs_ref, dq_ref, dk_ref, dv_ref,
    out_ref, whole_ref,
):
    columns = q_ref.shape[1]
    first = place()[1] == 0
    half = columns // DH // 2
    for h in range(columns // DH):
        c = slice(h * DH, (h + 1) * DH)
        own = first if h < half else jnp.logical_not(first)
        state, grad = (
            jnp.where(own, mine_ref[at : at + DH, :], theirs_ref[at : at + DH, :])
            for at in (h % half * DH, (half + h % half) * DH)
        )
        k, v, g = k_ref[:, c], v_ref[:, c], g_ref[:, c]
        lead, tail = lead_ref[:, c], tail_ref[:, c]
        dq = dq_ref[:, c] + lead * nt(g, state)
        dk = dk_ref[:, c] + tail * nt(v, grad)
        dv = dv_ref[:, c] + tail * nn(k, grad)
        for n, result in enumerate((dq, dk, dv)):
            whole_ref[:, pl.ds(n * columns + h * DH, DH)] = result.astype(BF16)
    for n in range(SIDE * SIDE):
        start = pl.multiple_of(member(n // SIDE, n % SIDE) * 16, 16)
        out_ref[pl.ds(n * 16, 16), :] = whole_ref[pl.ds(start, 16), :]


def inter(q, k, v, g, lead, tail, mine, theirs, within):
    rows, columns = q.shape
    return pl.pallas_call(
        inter_kernel,
        out_shape=pltpu.VMEM((rows, 3 * columns), BF16),
        in_specs=[VMEM] * 11,
        out_specs=VMEM,
        scratch_shapes=[pltpu.VMEM((rows, 3 * columns), BF16)],
        compiler_params=params(8),
        cost_estimate=cost(150_000_000, 6_000_000),
        name="inter",
    )(q, k, v, g, lead, tail, mine, theirs, *within)


def output_kernel(start, tile, d_ref, wq_ref, wk_ref, wv_ref, *refs):
    outs = refs[-SIDE:]
    rows = d_ref.shape[0]
    piece = rows // SIDE
    inner = wq_ref.shape[1]
    for n in range(outs[0].shape[1] // tile):
        total = jnp.zeros((rows, tile), F32)
        for part, w_ref in enumerate((wq_ref, wk_ref, wv_ref)):
            total += nt(
                d_ref[:, part * inner : (part + 1) * inner],
                w_ref[pl.ds(start + n * tile, tile), :],
            )
        c = slice(n * tile, (n + 1) * tile)
        for slot, out_ref in enumerate(outs):
            out_ref[:, c] = total[slot * piece : (slot + 1) * piece].astype(out_ref.dtype)


def output(d, weights, start, width, kinds, after=()):
    rows = d.shape[0]
    return pl.pallas_call(
        functools.partial(output_kernel, start, 512),
        out_shape=tuple(pltpu.VMEM((rows // SIDE, width), kind) for kind in kinds),
        in_specs=[VMEM] * (4 + len(after)),
        out_specs=(VMEM,) * SIDE,
        compiler_params=params(12),
        cost_estimate=cost(2 * rows * width * d.shape[1], 6_000_000),
        name="output",
    )(d, *weights, *after)


def relay_kernel(own_ref, other_ref, *refs):
    out_ref = refs[-1]
    out_ref[...] = (own_ref[...] + other_ref[...].astype(F32)).astype(BF16)


def relay(own, other, after=()):
    return pl.pallas_call(
        relay_kernel,
        out_shape=pltpu.VMEM(own.shape, BF16),
        in_specs=[VMEM] * (2 + len(after)),
        out_specs=VMEM,
        compiler_params=params(4),
        cost_estimate=cost(0, 100_000),
        name="relay",
    )(own, other, *after)


def total_of(own_ref, parts):
    total = own_ref[...]
    for ref in parts:
        total = total + ref[...].astype(F32)
    return total


def add_kernel(terms, *refs):
    own_ref, *parts = refs[:terms]
    earlier, outs = refs[terms:-SIDE], refs[-SIDE:]
    piece, width = outs[0].shape
    total = total_of(own_ref, parts)
    c = slice(width - own_ref.shape[1], width)
    for slot, out_ref in enumerate(outs):
        if earlier:
            out_ref[:, : c.start] = earlier[slot][...]
        out_ref[:, c] = total[slot * piece : (slot + 1) * piece].astype(out_ref.dtype)


def add(half, earlier=()):
    rows, width = half[0].shape
    piece = rows // SIDE
    width += earlier[0].shape[1] if earlier else 0
    return pl.pallas_call(
        functools.partial(add_kernel, len(half)),
        out_shape=(pltpu.VMEM((piece, width), F32),) + (pltpu.VMEM((piece, width), BF16),) * 3,
        in_specs=[VMEM] * (len(half) + len(earlier)),
        out_specs=(VMEM,) * SIDE,
        compiler_params=params(8),
        cost_estimate=cost(0, 500_000),
        name="add",
    )(*half, *earlier)


def finish_kernel(own_ref, a_ref, b_ref, c_ref, out_ref):
    out_ref[...] = total_of(own_ref, (a_ref, b_ref, c_ref)).astype(BF16)


def finish(own, parts):
    return pl.pallas_call(
        finish_kernel,
        out_shape=jax.ShapeDtypeStruct(own.shape, BF16),
        in_specs=[VMEM] * SIDE,
        out_specs=VMEM,
        compiler_params=params(8),
        cost_estimate=cost(500_000, 1_000_000),
        name="finish",
    )(own, *parts)


def near_move(array, offset):
    return move(array, plane_perm(True, offset))


def wide_move(array, offset):
    return move(array, plane_perm(False, offset))


def shards(features, w_query, w_key, w_value, log_decay, d_out):
    near = [near_move(features, -r) for r in REL[1:]]
    own, *weights = load((features, w_query, w_key), 48)
    top, low = join((own, *near), (weights[0],))
    weights, g = (*weights, w_value), d_out
    next_top, last_low = wide_move(top, -1), wide_move(low, 1)
    next_low, last_top = wide_move(low, -1), wide_move(top, 1)
    far_top, far_low = wide_move(next_top, -1), wide_move(last_low, 1)
    factors, lead, tail = decay_factors(log_decay)
    sums = project((top, low), (0,), None, weights, F32, (lead,))
    sums = project((next_top, next_low), (1,), sums, weights, F32)
    sums = project((last_top, last_low), (2,), sums, weights, F32)
    q, k, v = project((far_top, far_low), (3,), sums, weights, BF16)

    own_l, own_m, pay = states(q, k, v, g, lead, tail)
    peer = move(pay, core_perm())
    chip = chip_states(own_l, own_m, lead, peer)
    far = [move(p, chip_perm(d)) for d, p in enumerate(chip, 1)]
    within = intra(q, k, v, g, factors)
    mine, theirs = outer_states(own_l, own_m, lead, peer, far, within[:1])
    theirs = move(theirs, core_perm())
    d = inter(q, k, v, g, lead, tail, mine, theirs, within)

    width = w_query.shape[0] // HALVES
    a_own, a_next, a_last, a_far = output(d, weights, 0, width, (F32, F32, BF16, BF16))
    b_own, b_next, b_last, b_far = output(d, weights, width, width, (F32, BF16, F32, BF16), (a_own,))
    a_last, a_far = wide_move(a_last, -1), wide_move(a_far, 1)
    b_next, b_far = wide_move(b_next, 1), wide_move(b_far, -1)
    a_next = relay(a_next, a_far)
    b_last = relay(b_last, b_far, (a_next,))
    a_next, b_last = wide_move(a_next, 1), wide_move(b_last, -1)
    keep, *sends = add((b_own, b_next, b_last), add((a_own, a_last, a_next)))
    return finish(keep, [near_move(s, r) for s, r in zip(sends, REL[1:])])


def solution(mesh):
    return jax.shard_map(
        shards,
        mesh=mesh,
        in_specs=(
            P("ctx", "head"),
            P(None, "head"),
            P(None, "head"),
            P(None, "head"),
            P("head", "ctx"),
            P("ctx", "head"),
        ),
        out_specs=P(("ctx", "head"), None),
        check_vma=False,
    )
```

```python
import functools

import jax
import jax.numpy as jnp
from jax import lax
from jax.experimental import pallas as pl
from jax.experimental.pallas import tpu as pltpu
from jax.sharding import PartitionSpec as P

F32, BF16 = jnp.float32, jnp.bfloat16
HI = lax.Precision.HIGHEST
AXES = ("ctx", "head")
REL = (0, 1, 3, 2)
SIDE = 4
DH = 128
MIB = 2**20
VMEM = pl.BlockSpec(memory_space=pltpu.VMEM)
HBM = pl.BlockSpec(memory_space=pltpu.HBM)
HALVES = 2


def device(x, core, z, y):
    return (x * 2 + core) * 16 + z * 4 + y


def everywhere():
    for x in range(4):
        for core in range(2):
            for z in range(4):
                for y in range(4):
                    yield x, core, z, y


def plane_perm(first, offset):
    pairs = []
    for x, core, z, y in everywhere():
        along_y = (core == 0) == first
        to = (z, (y + offset) % 4) if along_y else ((z + offset) % 4, y)
        pairs.append((device(x, core, z, y), device(x, core, *to)))
    return pairs


def core_perm():
    return [(device(x, c, z, y), device(x, 1 - c, z, y)) for x, c, z, y in everywhere()]


def chip_perm(offset):
    return [
        (device(x, c, z, y), device((x + offset) % 4, c, z, y)) for x, c, z, y in everywhere()
    ]


def move(array, pairs):
    return lax.ppermute(array, AXES, pairs)


def place():
    ctx, head = lax.axis_index("ctx"), lax.axis_index("head")
    return ctx >> 1, ctx & 1, head >> 2, head & 3


def member(slot, inner):
    _, core, z, y = place()
    first = core == 0
    z = (z + jnp.where(first, REL[slot], REL[inner])) & 3
    y = (y + jnp.where(first, REL[inner], REL[slot])) & 3
    return z * 4 + y


def params(mib):
    return pltpu.CompilerParams(vmem_limit_bytes=mib * MIB)


def cost(flops, moved):
    return pl.CostEstimate(flops=flops, bytes_accessed=moved, transcendentals=0)


def nt(a, b):
    return lax.dot_general(a, b, (((1,), (1,)), ((), ())), preferred_element_type=F32)


def tn(a, b):
    return lax.dot_general(a, b, (((0,), (0,)), ((), ())), preferred_element_type=F32)


def nn(a, b):
    return jnp.dot(a, b, preferred_element_type=F32)


def decay_kernel(decay_ref, weights_ref, lead_ref, tail_ref):
    heads, rows = decay_ref.shape
    decay = decay_ref[...]
    row = lax.broadcasted_iota(jnp.int32, (rows, rows), 0)
    column = lax.broadcasted_iota(jnp.int32, (rows, rows), 1)
    causal = column <= row
    lower = jnp.where(causal, 1.0, 0.0)
    upright = lax.dot_general(
        lower, decay, (((1,), (1,)), ((), ())), precision=HI, preferred_element_type=F32
    )
    flat = lax.dot_general(
        decay, lower, (((1,), (1,)), ((), ())), precision=HI, preferred_element_type=F32
    )
    for h in range(heads):
        at_t = upright[:, h : h + 1]
        at_s = flat[h : h + 1, :]
        weights_ref[h] = jnp.where(causal, jnp.exp(jnp.minimum(at_t - at_s, 0.0)), 0.0)
        total = flat[h : h + 1, rows - 1 : rows]
        span = slice(h * DH, (h + 1) * DH)
        lead_ref[:, span] = jnp.broadcast_to(jnp.exp(at_t), (rows, DH))
        tail_ref[:, span] = jnp.broadcast_to(jnp.exp(total - at_t), (rows, DH))


def decay_factors(log_decay):
    heads, rows = log_decay.shape
    wide = pltpu.VMEM((rows, heads * DH), F32)
    return pl.pallas_call(
        decay_kernel,
        out_shape=(pltpu.VMEM((heads, rows, rows), F32), wide, wide),
        in_specs=[VMEM],
        out_specs=(VMEM, VMEM, VMEM),
        compiler_params=params(8),
        cost_estimate=cost(2_000_000, 2_000_000),
        name="decay",
    )(log_decay)


def load_kernel(*refs):
    count = len(refs) // 2
    sources, targets, done = refs[:count], refs[count:-1], refs[-1]
    pieces = done.shape[0] // count
    copies = []
    for n, (source, target) in enumerate(zip(sources, targets)):
        rows = source.shape[0] // pieces
        for i in range(pieces):
            at = pl.ds(i * rows, rows)
            copies.append(
                pltpu.make_async_copy(source.at[at], target.at[at], done.at[n * pieces + i])
            )
    for copy in copies:
        copy.start()
    for copy in copies:
        copy.wait()


def load(arrays, mib):
    moved = sum(2 * a.size * a.dtype.itemsize for a in arrays)
    return pl.pallas_call(
        load_kernel,
        out_shape=tuple(pltpu.VMEM(a.shape, a.dtype) for a in arrays),
        in_specs=[HBM] * len(arrays),
        out_specs=(VMEM,) * len(arrays),
        scratch_shapes=[pltpu.SemaphoreType.DMA((4 * len(arrays),))],
        compiler_params=params(mib),
        cost_estimate=cost(0, moved),
        name="load",
    )(*arrays)


def join_kernel(*refs):
    pieces, outs = refs[:SIDE], refs[-HALVES:]
    width = pieces[0].shape[1]
    for n, ref in enumerate(pieces):
        for m, out_ref in enumerate(outs):
            rows = out_ref.shape[0]
            out_ref[:, n * width : (n + 1) * width] = ref[m * rows : (m + 1) * rows, :]


def join(pieces, after):
    rows, width = pieces[0].shape
    return pl.pallas_call(
        join_kernel,
        out_shape=(pltpu.VMEM((rows // HALVES, SIDE * width), BF16),) * HALVES,
        in_specs=[VMEM] * (SIDE + len(after)),
        out_specs=(VMEM,) * HALVES,
        compiler_params=params(4),
        cost_estimate=cost(0, 2_000_000),
        name="join",
    )(*pieces, *after)


def project_kernel(slots, has_sum, *refs):
    count = HALVES * len(slots)
    xs, refs = refs[:count], refs[count:]
    sums, refs = (refs[:3], refs[3:]) if has_sum else (None, refs)
    weights, outs = refs[:3], refs[-3:]
    for n, (w_ref, out_ref) in enumerate(zip(weights, outs)):
        total = sums[n][...] if has_sum else None
        for m, slot in enumerate(slots):
            x = jnp.concatenate([r[...] for r in xs[m * HALVES : (m + 1) * HALVES]], axis=0)
            width = x.shape[1] // SIDE
            starts = [pl.multiple_of(member(slot, j) * width, 128) for j in range(SIDE)]
            w = jnp.concatenate([w_ref[pl.ds(s, width), :] for s in starts], axis=0)
            term = nn(x, w)
            total = term if total is None else total + term
        out_ref[...] = total.astype(out_ref.dtype)


def project(xs, slots, sums, weights, kind, after=()):
    rows, columns = HALVES * xs[0].shape[0], weights[0].shape[1]
    inner = xs[0].shape[1] * len(slots)
    has_sum = sums is not None
    return pl.pallas_call(
        functools.partial(project_kernel, slots, has_sum),
        out_shape=(pltpu.VMEM((rows, columns), kind),) * 3,
        in_specs=[VMEM] * (len(xs) + 3 + 3 * has_sum + len(after)),
        out_specs=(VMEM,) * 3,
        compiler_params=params(12),
        cost_estimate=cost(2 * 3 * rows * inner * columns, 4_000 * inner),
        name="project",
    )(*xs, *(sums or ()), *weights, *after)


def stack(lines):
    row = lax.broadcasted_iota(jnp.int32, (16, DH), 0)
    block = jnp.zeros((16, DH), F32)
    for n, line in enumerate(lines):
        block = jnp.where(row == n, line, block)
    return block.astype(BF16)


def line_of(ref, start, n):
    return ref[pl.ds(start, 16), :].astype(F32)[n : n + 1, :]


def states_kernel(q_ref, k_ref, v_ref, g_ref, lead_ref, tail_ref, l_ref, m_ref, pay_ref):
    rows, columns = q_ref.shape
    heads = columns // DH
    local, grad = [], []
    for h in range(heads):
        c = slice(h * DH, (h + 1) * DH)
        k = (k_ref[:, c].astype(F32) * tail_ref[:, c]).astype(BF16)
        q = (q_ref[:, c].astype(F32) * lead_ref[:, c]).astype(BF16)
        local.append(tn(k, v_ref[:, c]))
        grad.append(tn(q, g_ref[:, c]))
    first = place()[1] == 0
    half = heads // 2
    for i in range(half):
        s = slice(i * DH, (i + 1) * DH)
        for ref, state, at in ((l_ref, local, i), (m_ref, grad, half + i)):
            low, high = state[i], state[half + i]
            ref[s, :] = jnp.where(first, low, high)
            pay_ref[at * DH : (at + 1) * DH, :] = jnp.where(first, high, low).astype(BF16)
    pay_ref[pl.ds(columns, 16), :] = stack(
        [lead_ref[rows - 1 : rows, h * DH : (h + 1) * DH] for h in range(heads)]
    )


def states(q, k, v, g, lead, tail):
    columns = q.shape[1]
    state = pltpu.VMEM((columns // 2, DH), F32)
    return pl.pallas_call(
        states_kernel,
        out_shape=(state, state, pltpu.VMEM((columns + 16, DH), BF16)),
        in_specs=[VMEM] * 6,
        out_specs=(VMEM,) * 3,
        compiler_params=params(8),
        cost_estimate=cost(70_000_000, 3_000_000),
        name="states",
    )(q, k, v, g, lead, tail)


def intra_kernel(q_ref, k_ref, v_ref, g_ref, weights_ref, dq_ref, dk_ref, dv_ref):
    for h in range(q_ref.shape[1] // DH):
        c = slice(h * DH, (h + 1) * DH)
        q, k, v, g = q_ref[:, c], k_ref[:, c], v_ref[:, c], g_ref[:, c]
        weights = weights_ref[h]
        scores = (nt(q, k) * weights).astype(BF16)
        mixing = (nt(g, v) * weights).astype(BF16)
        dq_ref[:, c] = nn(mixing, k)
        dk_ref[:, c] = tn(mixing, q)
        dv_ref[:, c] = tn(scores, g)


def intra(q, k, v, g, weights):
    out = pltpu.VMEM(q.shape, F32)
    return pl.pallas_call(
        intra_kernel,
        out_shape=(out,) * 3,
        in_specs=[VMEM] * 5,
        out_specs=(VMEM,) * 3,
        compiler_params=params(8),
        cost_estimate=cost(340_000_000, 4_000_000),
        name="intra",
    )(q, k, v, g, weights)


def pair_of(l_ref, m_ref, lead_ref, peer_ref):
    columns, rows = peer_ref.shape[0] - 16, lead_ref.shape[0]
    half = columns // DH // 2
    first = place()[1] == 0
    for i in range(half):
        s = slice(i * DH, (i + 1) * DH)
        own, other = (
            jnp.where(first, line(i), line(half + i))
            for line in (
                lambda h: lead_ref[rows - 1 : rows, h * DH : (h + 1) * DH],
                lambda h: line_of(peer_ref, columns, h),
            )
        )
        peer_l = peer_ref[s, :].astype(F32)
        peer_m = peer_ref[(half + i) * DH : (half + i + 1) * DH, :].astype(F32)
        yield i, (l_ref[s, :], peer_l), (m_ref[s, :], peer_m), (own, other)


def chip_kernel(l_ref, m_ref, lead_ref, peer_ref, *pays):
    x, core, _, _ = place()
    first = core == 0
    decays = []
    rows = pays[0].shape[0] - 16
    for i, (own_l, peer_l), (own_m, peer_m), (own, other) in pair_of(l_ref, m_ref, lead_ref, peer_ref):
        chip_l = jnp.where(first, other * own_l + peer_l, own * peer_l + own_l)
        chip_m = jnp.where(first, own_m + own * peer_m, peer_m + other * own_m)
        decays.append(own * other)
        for d, pay_ref in enumerate(pays, 1):
            both = jnp.where(x + d < 4, chip_l, chip_m)
            pay_ref[i * DH : (i + 1) * DH, :] = both.astype(BF16)
    for pay_ref in pays:
        pay_ref[pl.ds(rows, 16), :] = stack(decays)


def chip_states(own_l, own_m, lead, peer):
    pay = pltpu.VMEM((own_l.shape[0] + 16, DH), BF16)
    return pl.pallas_call(
        chip_kernel,
        out_shape=(pay,) * 3,
        in_specs=[VMEM] * 4,
        out_specs=(VMEM,) * 3,
        compiler_params=params(8),
        cost_estimate=cost(500_000, 1_000_000),
        name="chip_states",
    )(own_l, own_m, lead, peer)


def outer_kernel(l_ref, m_ref, lead_ref, peer_ref, one_ref, two_ref, three_ref, *refs):
    mine_ref, theirs_ref = refs[-2:]
    x, core, _, _ = place()
    first = core == 0
    far = (one_ref, two_ref, three_ref)
    rows = one_ref.shape[0] - 16

    def chance(condition):
        return jnp.where(condition, 1.0, 0.0).astype(F32)

    for i, (own_l, peer_l), (own_m, peer_m), (own, other) in pair_of(l_ref, m_ref, lead_ref, peer_ref):
        s = slice(i * DH, (i + 1) * DH)
        one, two, three = (r[s, :].astype(F32) for r in far)
        d_one, _, d_three = (line_of(r, rows, i) for r in far)
        d_two = line_of(two_ref, rows, i)
        before = (
            chance(x >= 1) * one
            + (chance(x >= 2) * d_one) * two
            + (chance(x >= 3) * d_one * d_two) * three
        )
        after = (
            chance(x <= 2) * three
            + (chance(x <= 1) * d_three) * two
            + (chance(x <= 0) * d_three * d_two) * one
        )
        low_decay, high_decay = jnp.where(first, own, other), jnp.where(first, other, own)
        low_l, high_m = jnp.where(first, own_l, peer_l), jnp.where(first, peer_m, own_m)
        low = (before, high_decay * after + high_m)
        high = (low_decay * before + low_l, after)
        for n in range(2):
            at = slice(n * rows + i * DH, n * rows + (i + 1) * DH)
            mine_ref[at, :] = jnp.where(first, low[n], high[n]).astype(BF16)
            theirs_ref[at, :] = jnp.where(first, high[n], low[n]).astype(BF16)


def outer_states(own_l, own_m, lead, peer, far, after):
    out = pltpu.VMEM((2 * own_l.shape[0], DH), BF16)
    return pl.pallas_call(
        outer_kernel,
        out_shape=(out, out),
        in_specs=[VMEM] * (7 + len(after)),
        out_specs=(VMEM,) * 2,
        compiler_params=params(8),
        cost_estimate=cost(500_000, 1_000_000),
        name="outer_states",
    )(own_l, own_m, lead, peer, *far, *after)


def columns_of(core, columns, i):
    return pl.ds(pl.multiple_of(core * (columns // 2) + i * DH, DH), DH)


def inter_terms(refs, states_ref, c, i):
    k_ref, v_ref, g_ref, lead_ref, tail_ref, dq_ref, dk_ref, dv_ref = refs
    half = states_ref.shape[0] // 2
    state = states_ref[i * DH : (i + 1) * DH, :]
    grad = states_ref[half + i * DH : half + (i + 1) * DH, :]
    lead, tail = lead_ref[:, c], tail_ref[:, c]
    return (
        (dq_ref[:, c] + lead * nt(g_ref[:, c], state)).astype(BF16),
        (dk_ref[:, c] + tail * nt(v_ref[:, c], grad)).astype(BF16),
        (dv_ref[:, c] + tail * nn(k_ref[:, c], grad)).astype(BF16),
    )


def inter_own_kernel(*refs):
    refs, states_ref, out_ref = refs[:8], refs[8], refs[9]
    columns = refs[0].shape[1]
    core = place()[1]
    for i in range(columns // DH // 2):
        results = inter_terms(refs, states_ref, columns_of(core, columns, i), i)
        for n, result in enumerate(results):
            at = n * (columns // 2) + i * DH
            out_ref[:, at : at + DH] = result


def inter_kernel(*refs):
    refs, states_ref, own_ref, out_ref, whole_ref = refs[:8], refs[8], refs[9], refs[10], refs[11]
    columns = refs[0].shape[1]
    core = place()[1]
    for i in range(columns // DH // 2):
        results = inter_terms(refs, states_ref, columns_of(1 - core, columns, i), i)
        for n, result in enumerate(results):
            at = pl.multiple_of(n * columns + (1 - core) * (columns // 2) + i * DH, DH)
            whole_ref[:, pl.ds(at, DH)] = result
    for n in range(3):
        at = pl.multiple_of(n * columns + core * (columns // 2), DH)
        own = slice(n * (columns // 2), (n + 1) * (columns // 2))
        whole_ref[:, pl.ds(at, columns // 2)] = own_ref[:, own]
    for n in range(SIDE * SIDE):
        start = pl.multiple_of(member(n // SIDE, n % SIDE) * 16, 16)
        out_ref[pl.ds(n * 16, 16), :] = whole_ref[pl.ds(start, 16), :]


def inter_own(k, v, g, lead, tail, within, states):
    rows, columns = k.shape
    return pl.pallas_call(
        inter_own_kernel,
        out_shape=pltpu.VMEM((rows, 3 * columns // 2), BF16),
        in_specs=[VMEM] * 9,
        out_specs=VMEM,
        compiler_params=params(8),
        cost_estimate=cost(75_000_000, 3_000_000),
        name="inter_own",
    )(k, v, g, lead, tail, *within, states)


def inter(k, v, g, lead, tail, within, states, own):
    rows, columns = k.shape
    return pl.pallas_call(
        inter_kernel,
        out_shape=pltpu.VMEM((rows, 3 * columns), BF16),
        in_specs=[VMEM] * 10,
        out_specs=VMEM,
        scratch_shapes=[pltpu.VMEM((rows, 3 * columns), BF16)],
        compiler_params=params(8),
        cost_estimate=cost(75_000_000, 4_000_000),
        name="inter",
    )(k, v, g, lead, tail, *within, states, own)


def output_kernel(start, tile, d_ref, wq_ref, wk_ref, wv_ref, *refs):
    outs = refs[-SIDE:]
    rows = d_ref.shape[0]
    piece = rows // SIDE
    inner = wq_ref.shape[1]
    for n in range(outs[0].shape[1] // tile):
        total = jnp.zeros((rows, tile), F32)
        for part, w_ref in enumerate((wq_ref, wk_ref, wv_ref)):
            total += nt(
                d_ref[:, part * inner : (part + 1) * inner],
                w_ref[pl.ds(start + n * tile, tile), :],
            )
        c = slice(n * tile, (n + 1) * tile)
        for slot, out_ref in enumerate(outs):
            out_ref[:, c] = total[slot * piece : (slot + 1) * piece].astype(out_ref.dtype)


def output(d, weights, start, width, kinds, after=()):
    rows = d.shape[0]
    return pl.pallas_call(
        functools.partial(output_kernel, start, 512),
        out_shape=tuple(pltpu.VMEM((rows // SIDE, width), kind) for kind in kinds),
        in_specs=[VMEM] * (4 + len(after)),
        out_specs=(VMEM,) * SIDE,
        compiler_params=params(12),
        cost_estimate=cost(2 * rows * width * d.shape[1], 6_000_000),
        name="output",
    )(d, *weights, *after)


def relay_kernel(own_ref, other_ref, *refs):
    out_ref = refs[-1]
    out_ref[...] = (own_ref[...] + other_ref[...].astype(F32)).astype(BF16)


def relay(own, other, after=()):
    return pl.pallas_call(
        relay_kernel,
        out_shape=pltpu.VMEM(own.shape, BF16),
        in_specs=[VMEM] * (2 + len(after)),
        out_specs=VMEM,
        compiler_params=params(4),
        cost_estimate=cost(0, 100_000),
        name="relay",
    )(own, other, *after)


def total_of(own_ref, parts):
    total = own_ref[...]
    for ref in parts:
        total = total + ref[...].astype(F32)
    return total


def add_kernel(terms, *refs):
    own_ref, *parts = refs[:terms]
    earlier, outs = refs[terms:-SIDE], refs[-SIDE:]
    piece, width = outs[0].shape
    total = total_of(own_ref, parts)
    c = slice(width - own_ref.shape[1], width)
    for slot, out_ref in enumerate(outs):
        if earlier:
            out_ref[:, : c.start] = earlier[slot][...]
        out_ref[:, c] = total[slot * piece : (slot + 1) * piece].astype(out_ref.dtype)


def add(half, earlier=()):
    rows, width = half[0].shape
    piece = rows // SIDE
    width += earlier[0].shape[1] if earlier else 0
    return pl.pallas_call(
        functools.partial(add_kernel, len(half)),
        out_shape=(pltpu.VMEM((piece, width), F32),) + (pltpu.VMEM((piece, width), BF16),) * 3,
        in_specs=[VMEM] * (len(half) + len(earlier)),
        out_specs=(VMEM,) * SIDE,
        compiler_params=params(8),
        cost_estimate=cost(0, 500_000),
        name="add",
    )(*half, *earlier)


def finish_kernel(own_ref, a_ref, b_ref, c_ref, out_ref):
    out_ref[...] = total_of(own_ref, (a_ref, b_ref, c_ref)).astype(BF16)


def finish(own, parts):
    return pl.pallas_call(
        finish_kernel,
        out_shape=jax.ShapeDtypeStruct(own.shape, BF16),
        in_specs=[VMEM] * SIDE,
        out_specs=VMEM,
        compiler_params=params(8),
        cost_estimate=cost(500_000, 1_000_000),
        name="finish",
    )(own, *parts)


def near_move(array, offset):
    return move(array, plane_perm(True, offset))


def wide_move(array, offset):
    return move(array, plane_perm(False, offset))


def shards(features, w_query, w_key, w_value, log_decay, d_out):
    near = [near_move(features, -r) for r in REL[1:]]
    own, *weights = load((features, w_query, w_key), 48)
    top, low = join((own, *near), (weights[0],))
    weights, g = (*weights, w_value), d_out
    next_top, last_low = wide_move(top, -1), wide_move(low, 1)
    next_low, last_top = wide_move(low, -1), wide_move(top, 1)
    far_top, far_low = wide_move(next_top, -1), wide_move(last_low, 1)
    factors, lead, tail = decay_factors(log_decay)
    sums = project((top, low), (0,), None, weights, F32, (lead,))
    sums = project((next_top, next_low), (1,), sums, weights, F32)
    sums = project((last_top, last_low), (2,), sums, weights, F32)
    q, k, v = project((far_top, far_low), (3,), sums, weights, BF16)

    own_l, own_m, pay = states(q, k, v, g, lead, tail)
    peer = move(pay, core_perm())
    chip = chip_states(own_l, own_m, lead, peer)
    far = [move(p, chip_perm(d)) for d, p in enumerate(chip, 1)]
    within = intra(q, k, v, g, factors)
    mine, theirs = outer_states(own_l, own_m, lead, peer, far, within[:1])
    theirs = move(theirs, core_perm())
    ready = inter_own(k, v, g, lead, tail, within, mine)
    d = inter(k, v, g, lead, tail, within, theirs, ready)

    width = w_query.shape[0] // HALVES
    a_own, a_next, a_last, a_far = output(d, weights, 0, width, (F32, F32, BF16, BF16))
    b_own, b_next, b_last, b_far = output(d, weights, width, width, (F32, BF16, F32, BF16), (a_own,))
    a_last, a_far = wide_move(a_last, -1), wide_move(a_far, 1)
    b_next, b_far = wide_move(b_next, 1), wide_move(b_far, -1)
    a_next = relay(a_next, a_far)
    b_last = relay(b_last, b_far, (a_next,))
    a_next, b_last = wide_move(a_next, 1), wide_move(b_last, -1)
    keep, *sends = add((b_own, b_next, b_last), add((a_own, a_last, a_next)))
    return finish(keep, [near_move(s, r) for s, r in zip(sends, REL[1:])])


def solution(mesh):
    return jax.shard_map(
        shards,
        mesh=mesh,
        in_specs=(
            P("ctx", "head"),
            P(None, "head"),
            P(None, "head"),
            P(None, "head"),
            P("head", "ctx"),
            P("ctx", "head"),
        ),
        out_specs=P(("ctx", "head"), None),
        check_vma=False,
    )
```

```python
import functools

import jax
import jax.numpy as jnp
from jax import lax
from jax.experimental import pallas as pl
from jax.experimental.pallas import tpu as pltpu
from jax.sharding import PartitionSpec as P

F32, BF16 = jnp.float32, jnp.bfloat16
HI = lax.Precision.HIGHEST
AXES = ("ctx", "head")
REL = (0, 1, 3, 2)
SIDE = 4
DH = 128
MIB = 2**20
VMEM = pl.BlockSpec(memory_space=pltpu.VMEM)
HBM = pl.BlockSpec(memory_space=pltpu.HBM)
HALVES = 2


def device(x, core, z, y):
    return (x * 2 + core) * 16 + z * 4 + y


def everywhere():
    for x in range(4):
        for core in range(2):
            for z in range(4):
                for y in range(4):
                    yield x, core, z, y


def plane_perm(first, offset):
    pairs = []
    for x, core, z, y in everywhere():
        along_y = (core == 0) == first
        to = (z, (y + offset) % 4) if along_y else ((z + offset) % 4, y)
        pairs.append((device(x, core, z, y), device(x, core, *to)))
    return pairs


def core_perm():
    return [(device(x, c, z, y), device(x, 1 - c, z, y)) for x, c, z, y in everywhere()]


def chip_perm(offset):
    return [
        (device(x, c, z, y), device((x + offset) % 4, c, z, y)) for x, c, z, y in everywhere()
    ]


def move(array, pairs):
    return lax.ppermute(array, AXES, pairs)


def place():
    ctx, head = lax.axis_index("ctx"), lax.axis_index("head")
    return ctx >> 1, ctx & 1, head >> 2, head & 3


def member(slot, inner):
    _, core, z, y = place()
    first = core == 0
    z = (z + jnp.where(first, REL[slot], REL[inner])) & 3
    y = (y + jnp.where(first, REL[inner], REL[slot])) & 3
    return z * 4 + y


def params(mib):
    return pltpu.CompilerParams(vmem_limit_bytes=mib * MIB)


def cost(flops, moved):
    return pl.CostEstimate(flops=flops, bytes_accessed=moved, transcendentals=0)


def nt(a, b):
    return lax.dot_general(a, b, (((1,), (1,)), ((), ())), preferred_element_type=F32)


def tn(a, b):
    return lax.dot_general(a, b, (((0,), (0,)), ((), ())), preferred_element_type=F32)


def nn(a, b):
    return jnp.dot(a, b, preferred_element_type=F32)


def decay_kernel(decay_ref, weights_ref, lead_ref, tail_ref):
    heads, rows = decay_ref.shape
    decay = decay_ref[...]
    row = lax.broadcasted_iota(jnp.int32, (rows, rows), 0)
    column = lax.broadcasted_iota(jnp.int32, (rows, rows), 1)
    causal = column <= row
    lower = jnp.where(causal, 1.0, 0.0)
    upright = lax.dot_general(
        lower, decay, (((1,), (1,)), ((), ())), precision=HI, preferred_element_type=F32
    )
    flat = lax.dot_general(
        decay, lower, (((1,), (1,)), ((), ())), precision=HI, preferred_element_type=F32
    )
    for h in range(heads):
        at_t = upright[:, h : h + 1]
        at_s = flat[h : h + 1, :]
        weights_ref[h] = jnp.where(causal, jnp.exp(jnp.minimum(at_t - at_s, 0.0)), 0.0)
        total = flat[h : h + 1, rows - 1 : rows]
        span = slice(h * DH, (h + 1) * DH)
        lead_ref[:, span] = jnp.broadcast_to(jnp.exp(at_t), (rows, DH))
        tail_ref[:, span] = jnp.broadcast_to(jnp.exp(total - at_t), (rows, DH))


def decay_factors(log_decay):
    heads, rows = log_decay.shape
    wide = pltpu.VMEM((rows, heads * DH), F32)
    return pl.pallas_call(
        decay_kernel,
        out_shape=(pltpu.VMEM((heads, rows, rows), F32), wide, wide),
        in_specs=[VMEM],
        out_specs=(VMEM, VMEM, VMEM),
        compiler_params=params(8),
        cost_estimate=cost(2_000_000, 2_000_000),
        name="decay",
    )(log_decay)


def load_kernel(*refs):
    count = len(refs) // 2
    sources, targets, done = refs[:count], refs[count:-1], refs[-1]
    pieces = done.shape[0] // count
    copies = []
    for n, (source, target) in enumerate(zip(sources, targets)):
        rows = source.shape[0] // pieces
        for i in range(pieces):
            at = pl.ds(i * rows, rows)
            copies.append(
                pltpu.make_async_copy(source.at[at], target.at[at], done.at[n * pieces + i])
            )
    for copy in copies:
        copy.start()
    for copy in copies:
        copy.wait()


def load(arrays, mib):
    moved = sum(2 * a.size * a.dtype.itemsize for a in arrays)
    return pl.pallas_call(
        load_kernel,
        out_shape=tuple(pltpu.VMEM(a.shape, a.dtype) for a in arrays),
        in_specs=[HBM] * len(arrays),
        out_specs=(VMEM,) * len(arrays),
        scratch_shapes=[pltpu.SemaphoreType.DMA((4 * len(arrays),))],
        compiler_params=params(mib),
        cost_estimate=cost(0, moved),
        name="load",
    )(*arrays)


def join_kernel(*refs):
    pieces, outs = refs[:SIDE], refs[-HALVES:]
    width = pieces[0].shape[1]
    for n, ref in enumerate(pieces):
        for m, out_ref in enumerate(outs):
            rows = out_ref.shape[0]
            out_ref[:, n * width : (n + 1) * width] = ref[m * rows : (m + 1) * rows, :]


def join(pieces, after):
    rows, width = pieces[0].shape
    return pl.pallas_call(
        join_kernel,
        out_shape=(pltpu.VMEM((rows // HALVES, SIDE * width), BF16),) * HALVES,
        in_specs=[VMEM] * (SIDE + len(after)),
        out_specs=(VMEM,) * HALVES,
        compiler_params=params(4),
        cost_estimate=cost(0, 2_000_000),
        name="join",
    )(*pieces, *after)


def project_kernel(slots, has_sum, *refs):
    count = HALVES * len(slots)
    xs, refs = refs[:count], refs[count:]
    sums, refs = (refs[:3], refs[3:]) if has_sum else (None, refs)
    weights, outs = refs[:3], refs[-3:]
    for n, (w_ref, out_ref) in enumerate(zip(weights, outs)):
        total = sums[n][...] if has_sum else None
        for m, slot in enumerate(slots):
            x = jnp.concatenate([r[...] for r in xs[m * HALVES : (m + 1) * HALVES]], axis=0)
            width = x.shape[1] // SIDE
            starts = [pl.multiple_of(member(slot, j) * width, 128) for j in range(SIDE)]
            w = jnp.concatenate([w_ref[pl.ds(s, width), :] for s in starts], axis=0)
            term = nn(x, w)
            total = term if total is None else total + term
        out_ref[...] = total.astype(out_ref.dtype)


def project(xs, slots, sums, weights, kind, after=()):
    rows, columns = HALVES * xs[0].shape[0], weights[0].shape[1]
    inner = xs[0].shape[1] * len(slots)
    has_sum = sums is not None
    return pl.pallas_call(
        functools.partial(project_kernel, slots, has_sum),
        out_shape=(pltpu.VMEM((rows, columns), kind),) * 3,
        in_specs=[VMEM] * (len(xs) + 3 + 3 * has_sum + len(after)),
        out_specs=(VMEM,) * 3,
        compiler_params=params(12),
        cost_estimate=cost(2 * 3 * rows * inner * columns, 4_000 * inner),
        name="project",
    )(*xs, *(sums or ()), *weights, *after)


def stack(lines):
    row = lax.broadcasted_iota(jnp.int32, (16, DH), 0)
    block = jnp.zeros((16, DH), F32)
    for n, line in enumerate(lines):
        block = jnp.where(row == n, line, block)
    return block.astype(BF16)


def line_of(ref, start, n):
    return ref[pl.ds(start, 16), :].astype(F32)[n : n + 1, :]


def states_kernel(q_ref, k_ref, v_ref, g_ref, lead_ref, tail_ref, l_ref, m_ref, pay_ref):
    rows, columns = q_ref.shape
    heads = columns // DH
    local, grad = [], []
    for h in range(heads):
        c = slice(h * DH, (h + 1) * DH)
        k = (k_ref[:, c].astype(F32) * tail_ref[:, c]).astype(BF16)
        q = (q_ref[:, c].astype(F32) * lead_ref[:, c]).astype(BF16)
        local.append(tn(k, v_ref[:, c]))
        grad.append(tn(q, g_ref[:, c]))
    first = place()[1] == 0
    half = heads // 2
    for i in range(half):
        s = slice(i * DH, (i + 1) * DH)
        for ref, state, at in ((l_ref, local, i), (m_ref, grad, half + i)):
            low, high = state[i], state[half + i]
            ref[s, :] = jnp.where(first, low, high)
            pay_ref[at * DH : (at + 1) * DH, :] = jnp.where(first, high, low).astype(BF16)
    pay_ref[pl.ds(columns, 16), :] = stack(
        [lead_ref[rows - 1 : rows, h * DH : (h + 1) * DH] for h in range(heads)]
    )


def states(q, k, v, g, lead, tail):
    columns = q.shape[1]
    state = pltpu.VMEM((columns // 2, DH), F32)
    return pl.pallas_call(
        states_kernel,
        out_shape=(state, state, pltpu.VMEM((columns + 16, DH), BF16)),
        in_specs=[VMEM] * 6,
        out_specs=(VMEM,) * 3,
        compiler_params=params(8),
        cost_estimate=cost(70_000_000, 3_000_000),
        name="states",
    )(q, k, v, g, lead, tail)


def intra_kernel(q_ref, k_ref, v_ref, g_ref, weights_ref, dq_ref, dk_ref, dv_ref):
    for h in range(q_ref.shape[1] // DH):
        c = slice(h * DH, (h + 1) * DH)
        q, k, v, g = q_ref[:, c], k_ref[:, c], v_ref[:, c], g_ref[:, c]
        weights = weights_ref[h]
        scores = (nt(q, k) * weights).astype(BF16)
        mixing = (nt(g, v) * weights).astype(BF16)
        dq_ref[:, c] = nn(mixing, k)
        dk_ref[:, c] = tn(mixing, q)
        dv_ref[:, c] = tn(scores, g)


def intra(q, k, v, g, weights):
    out = pltpu.VMEM(q.shape, F32)
    return pl.pallas_call(
        intra_kernel,
        out_shape=(out,) * 3,
        in_specs=[VMEM] * 5,
        out_specs=(VMEM,) * 3,
        compiler_params=params(8),
        cost_estimate=cost(340_000_000, 4_000_000),
        name="intra",
    )(q, k, v, g, weights)


def pair_of(l_ref, m_ref, lead_ref, peer_ref):
    columns, rows = peer_ref.shape[0] - 16, lead_ref.shape[0]
    half = columns // DH // 2
    first = place()[1] == 0
    for i in range(half):
        s = slice(i * DH, (i + 1) * DH)
        own, other = (
            jnp.where(first, line(i), line(half + i))
            for line in (
                lambda h: lead_ref[rows - 1 : rows, h * DH : (h + 1) * DH],
                lambda h: line_of(peer_ref, columns, h),
            )
        )
        peer_l = peer_ref[s, :].astype(F32)
        peer_m = peer_ref[(half + i) * DH : (half + i + 1) * DH, :].astype(F32)
        yield i, (l_ref[s, :], peer_l), (m_ref[s, :], peer_m), (own, other)


def chip_kernel(l_ref, m_ref, lead_ref, peer_ref, *pays):
    x, core, _, _ = place()
    first = core == 0
    decays = []
    rows = pays[0].shape[0] - 16
    for i, (own_l, peer_l), (own_m, peer_m), (own, other) in pair_of(l_ref, m_ref, lead_ref, peer_ref):
        chip_l = jnp.where(first, other * own_l + peer_l, own * peer_l + own_l)
        chip_m = jnp.where(first, own_m + own * peer_m, peer_m + other * own_m)
        decays.append(own * other)
        for d, pay_ref in enumerate(pays, 1):
            both = jnp.where(x + d < 4, chip_l, chip_m)
            pay_ref[i * DH : (i + 1) * DH, :] = both.astype(BF16)
    for pay_ref in pays:
        pay_ref[pl.ds(rows, 16), :] = stack(decays)


def chip_states(own_l, own_m, lead, peer):
    pay = pltpu.VMEM((own_l.shape[0] + 16, DH), BF16)
    return pl.pallas_call(
        chip_kernel,
        out_shape=(pay,) * 3,
        in_specs=[VMEM] * 4,
        out_specs=(VMEM,) * 3,
        compiler_params=params(8),
        cost_estimate=cost(500_000, 1_000_000),
        name="chip_states",
    )(own_l, own_m, lead, peer)


def outer_kernel(l_ref, m_ref, lead_ref, peer_ref, one_ref, two_ref, three_ref, *refs):
    mine_ref, theirs_ref = refs[-2:]
    x, core, _, _ = place()
    first = core == 0
    far = (one_ref, two_ref, three_ref)
    rows = one_ref.shape[0] - 16

    def chance(condition):
        return jnp.where(condition, 1.0, 0.0).astype(F32)

    for i, (own_l, peer_l), (own_m, peer_m), (own, other) in pair_of(l_ref, m_ref, lead_ref, peer_ref):
        s = slice(i * DH, (i + 1) * DH)
        one, two, three = (r[s, :].astype(F32) for r in far)
        d_one, _, d_three = (line_of(r, rows, i) for r in far)
        d_two = line_of(two_ref, rows, i)
        before = (
            chance(x >= 1) * one
            + (chance(x >= 2) * d_one) * two
            + (chance(x >= 3) * d_one * d_two) * three
        )
        after = (
            chance(x <= 2) * three
            + (chance(x <= 1) * d_three) * two
            + (chance(x <= 0) * d_three * d_two) * one
        )
        low_decay, high_decay = jnp.where(first, own, other), jnp.where(first, other, own)
        low_l, high_m = jnp.where(first, own_l, peer_l), jnp.where(first, peer_m, own_m)
        low = (before, high_decay * after + high_m)
        high = (low_decay * before + low_l, after)
        for n in range(2):
            at = slice(n * rows + i * DH, n * rows + (i + 1) * DH)
            mine_ref[at, :] = jnp.where(first, low[n], high[n]).astype(BF16)
            theirs_ref[at, :] = jnp.where(first, high[n], low[n]).astype(BF16)


def outer_states(own_l, own_m, lead, peer, far, after):
    out = pltpu.VMEM((2 * own_l.shape[0], DH), BF16)
    return pl.pallas_call(
        outer_kernel,
        out_shape=(out, out),
        in_specs=[VMEM] * (7 + len(after)),
        out_specs=(VMEM,) * 2,
        compiler_params=params(8),
        cost_estimate=cost(500_000, 1_000_000),
        name="outer_states",
    )(own_l, own_m, lead, peer, *far, *after)


def inter_kernel(
    q_ref, k_ref, v_ref, g_ref, lead_ref, tail_ref, mine_ref, theirs_ref, dq_ref, dk_ref, dv_ref,
    out_ref, whole_ref,
):
    columns = q_ref.shape[1]
    first = place()[1] == 0
    half = columns // DH // 2
    for h in range(columns // DH):
        c = slice(h * DH, (h + 1) * DH)
        own = first if h < half else jnp.logical_not(first)
        state, grad = (
            jnp.where(own, mine_ref[at : at + DH, :], theirs_ref[at : at + DH, :])
            for at in (h % half * DH, (half + h % half) * DH)
        )
        k, v, g = k_ref[:, c], v_ref[:, c], g_ref[:, c]
        lead, tail = lead_ref[:, c], tail_ref[:, c]
        dq = dq_ref[:, c] + lead * nt(g, state)
        dk = dk_ref[:, c] + tail * nt(v, grad)
        dv = dv_ref[:, c] + tail * nn(k, grad)
        for n, result in enumerate((dq, dk, dv)):
            whole_ref[:, pl.ds(n * columns + h * DH, DH)] = result.astype(BF16)
    for n in range(SIDE * SIDE):
        start = pl.multiple_of(member(n // SIDE, n % SIDE) * 16, 16)
        out_ref[pl.ds(n * 16, 16), :] = whole_ref[pl.ds(start, 16), :]


def inter(q, k, v, g, lead, tail, mine, theirs, within):
    rows, columns = q.shape
    return pl.pallas_call(
        inter_kernel,
        out_shape=pltpu.VMEM((rows, 3 * columns), BF16),
        in_specs=[VMEM] * 11,
        out_specs=VMEM,
        scratch_shapes=[pltpu.VMEM((rows, 3 * columns), BF16)],
        compiler_params=params(8),
        cost_estimate=cost(150_000_000, 6_000_000),
        name="inter",
    )(q, k, v, g, lead, tail, mine, theirs, *within)


def output_kernel(start, tile, d_ref, wq_ref, wk_ref, wv_ref, *refs):
    outs = refs[-SIDE:]
    rows = d_ref.shape[0]
    piece = rows // SIDE
    inner = wq_ref.shape[1]
    for n in range(outs[0].shape[1] // tile):
        total = jnp.zeros((rows, tile), F32)
        for part, w_ref in enumerate((wq_ref, wk_ref, wv_ref)):
            total += nt(
                d_ref[:, part * inner : (part + 1) * inner],
                w_ref[pl.ds(start + n * tile, tile), :],
            )
        c = slice(n * tile, (n + 1) * tile)
        for slot, out_ref in enumerate(outs):
            out_ref[:, c] = total[slot * piece : (slot + 1) * piece].astype(out_ref.dtype)


def output(d, weights, start, width, kinds, after=()):
    rows = d.shape[0]
    return pl.pallas_call(
        functools.partial(output_kernel, start, 1024),
        out_shape=tuple(pltpu.VMEM((rows // SIDE, width), kind) for kind in kinds),
        in_specs=[VMEM] * (4 + len(after)),
        out_specs=(VMEM,) * SIDE,
        compiler_params=params(12),
        cost_estimate=cost(2 * rows * width * d.shape[1], 6_000_000),
        name="output",
    )(d, *weights, *after)


def relay_kernel(own_ref, other_ref, *refs):
    out_ref = refs[-1]
    out_ref[...] = (own_ref[...] + other_ref[...].astype(F32)).astype(BF16)


def relay(own, other, after=()):
    return pl.pallas_call(
        relay_kernel,
        out_shape=pltpu.VMEM(own.shape, BF16),
        in_specs=[VMEM] * (2 + len(after)),
        out_specs=VMEM,
        compiler_params=params(4),
        cost_estimate=cost(0, 100_000),
        name="relay",
    )(own, other, *after)


def total_of(own_ref, parts):
    total = own_ref[...]
    for ref in parts:
        total = total + ref[...].astype(F32)
    return total


def add_kernel(terms, *refs):
    own_ref, *parts = refs[:terms]
    earlier, outs = refs[terms:-SIDE], refs[-SIDE:]
    piece, width = outs[0].shape
    total = total_of(own_ref, parts)
    c = slice(width - own_ref.shape[1], width)
    for slot, out_ref in enumerate(outs):
        if earlier:
            out_ref[:, : c.start] = earlier[slot][...]
        out_ref[:, c] = total[slot * piece : (slot + 1) * piece].astype(out_ref.dtype)


def add(half, earlier=()):
    rows, width = half[0].shape
    piece = rows // SIDE
    width += earlier[0].shape[1] if earlier else 0
    return pl.pallas_call(
        functools.partial(add_kernel, len(half)),
        out_shape=(pltpu.VMEM((piece, width), F32),) + (pltpu.VMEM((piece, width), BF16),) * 3,
        in_specs=[VMEM] * (len(half) + len(earlier)),
        out_specs=(VMEM,) * SIDE,
        compiler_params=params(8),
        cost_estimate=cost(0, 500_000),
        name="add",
    )(*half, *earlier)


def finish_kernel(own_ref, a_ref, b_ref, c_ref, out_ref):
    out_ref[...] = total_of(own_ref, (a_ref, b_ref, c_ref)).astype(BF16)


def finish(own, parts):
    return pl.pallas_call(
        finish_kernel,
        out_shape=jax.ShapeDtypeStruct(own.shape, BF16),
        in_specs=[VMEM] * SIDE,
        out_specs=VMEM,
        compiler_params=params(8),
        cost_estimate=cost(500_000, 1_000_000),
        name="finish",
    )(own, *parts)


def near_move(array, offset):
    return move(array, plane_perm(True, offset))


def wide_move(array, offset):
    return move(array, plane_perm(False, offset))


def shards(features, w_query, w_key, w_value, log_decay, d_out):
    near = [near_move(features, -r) for r in REL[1:]]
    own, *weights = load((features, w_query, w_key), 48)
    top, low = join((own, *near), (weights[0],))
    weights, g = (*weights, w_value), d_out
    next_top, last_low = wide_move(top, -1), wide_move(low, 1)
    next_low, last_top = wide_move(low, -1), wide_move(top, 1)
    far_top, far_low = wide_move(next_top, -1), wide_move(last_low, 1)
    factors, lead, tail = decay_factors(log_decay)
    sums = project((top, low), (0,), None, weights, F32, (lead,))
    sums = project((next_top, next_low), (1,), sums, weights, F32)
    sums = project((last_top, last_low), (2,), sums, weights, F32)
    q, k, v = project((far_top, far_low), (3,), sums, weights, BF16)

    own_l, own_m, pay = states(q, k, v, g, lead, tail)
    peer = move(pay, core_perm())
    chip = chip_states(own_l, own_m, lead, peer)
    far = [move(p, chip_perm(d)) for d, p in enumerate(chip, 1)]
    within = intra(q, k, v, g, factors)
    mine, theirs = outer_states(own_l, own_m, lead, peer, far, within[:1])
    theirs = move(theirs, core_perm())
    d = inter(q, k, v, g, lead, tail, mine, theirs, within)

    width = w_query.shape[0] // HALVES
    a_own, a_next, a_last, a_far = output(d, weights, 0, width, (F32, F32, BF16, BF16))
    b_own, b_next, b_last, b_far = output(d, weights, width, width, (F32, BF16, F32, BF16), (a_own,))
    a_last, a_far = wide_move(a_last, -1), wide_move(a_far, 1)
    b_next, b_far = wide_move(b_next, 1), wide_move(b_far, -1)
    a_next = relay(a_next, a_far)
    b_last = relay(b_last, b_far, (a_next,))
    a_next, b_last = wide_move(a_next, 1), wide_move(b_last, -1)
    keep, *sends = add((b_own, b_next, b_last), add((a_own, a_last, a_next)))
    return finish(keep, [near_move(s, r) for s, r in zip(sends, REL[1:])])


def solution(mesh):
    return jax.shard_map(
        shards,
        mesh=mesh,
        in_specs=(
            P("ctx", "head"),
            P(None, "head"),
            P(None, "head"),
            P(None, "head"),
            P("head", "ctx"),
            P("ctx", "head"),
        ),
        out_specs=P(("ctx", "head"), None),
        check_vma=False,
    )
```
